32 devices in a mesh: fr: 4 (over x, core), fc: 8 (over z, y).
Axes of the slice: x: 2, y: 2, z: 4, core: 2. Of those that a mesh axis runs over, the one named last changes fastest.
Arguments:
- front_slab: float32 [2048, 24576], P('fr', 'fc'), may hold values from -6 to 6
- panels: float32 [4, 24576, 256], P(None, 'fc'), may hold values from -8 to 8
- diagonal_blocks: float32 [4, 256, 256], P(None, None, 'fc'), may hold values from -3 to 96, as said below
- extend_maps: int32 [4, 4, 8, 128], P(None, 'fr', 'fc'), may hold values from 0 to 127, each once within a row
Outputs:
- front_out: float32 [2048, 24576], P('fr', 'fc')
The draws below stay inside these ranges and needn't reach their ends.
Inputs may be any that keep to these rules, and one draw needn't show every extreme that they name: `extend_maps`: each level's map at each grid position names every row of the block once. `diagonal_blocks`: the symmetric part of each block is positive definite.
All inputs are finite; a program needn't handle non-finite values.
Results may differ from the reference program's by a relative error of at most 0.0001.
Values sent between devices are 32-bit elements; how exact they have to be, the bound alone decides.
A program may use at most 128 MiB of HBM per device.

```python
import jax
import jax.numpy as jnp
import numpy as np
from jax import lax

LEVELS = 4
PW = 256
BLOCK = 128
CD = 3072
RD = 512
NT = 24576
SLAB = 2048
N_FR = 4
N_FC = 8


def draw_diagonal_blocks(key, part):
    key_values, key_scales = jax.random.split(jax.random.fold_in(key, 11))
    values = jnp.clip(jax.random.normal(key_values, (LEVELS, PW, PW), jnp.float32), -3.0, 3.0)
    scales = jax.random.uniform(key_scales, (LEVELS, PW), jnp.float32, 48.0, 96.0)
    identity = jnp.eye(PW, dtype=jnp.float32)
    return values * (1.0 - identity) + scales[:, None, :] * identity


def level_of(rng, shape, cuts, low, largest):
    loudness, own = 1.0, jax.random.fold_in(rng, 6)
    for dim, parts in cuts:
        draws = jnp.exp(jax.random.uniform(jax.random.fold_in(own, dim), (parts,), jnp.float32, low / len(cuts), largest / len(cuts)))
        loudness = loudness * jnp.repeat(draws, shape[dim] // parts).reshape([-1 if axis == dim else 1 for axis in range(len(shape))])
    return loudness


def noise(rng, extent, deviation, reach, pieces=(), kind=jnp.bfloat16):
    values = deviation * jax.random.normal(rng, extent, jnp.float32)
    if pieces:
        values = values * level_of(rng, extent, pieces, -0.22, 0.18)
    return jnp.clip(values, -reach, reach).astype(kind)


def setup_inputs(seed: int = 0) -> dict:
    keys = jax.random.split(jax.random.key(seed), 5)
    return {
        "front_slab": noise(keys[0], (SLAB, NT), 1.0, 6.0, ((0, 4), (1, 8)), jnp.float32),
        "panels": noise(keys[1], (LEVELS, NT, PW), 1.5, 8.0, ((1, 8),), jnp.float32),
        "diagonal_blocks": draw_diagonal_blocks(jax.random.fold_in(keys[4], 71), 0),
        "extend_maps": jax.vmap(lambda own: jax.random.permutation(own, BLOCK))(jax.random.split(keys[3], LEVELS * N_FR * N_FC)).reshape((LEVELS, N_FR, N_FC, BLOCK)).astype(jnp.int32),
    }


HIGHEST = lax.Precision.HIGHEST

def inverse_factor(diagonal_block):
    symmetric = 0.5 * (diagonal_block + diagonal_block.T)
    lower_factor = jnp.linalg.cholesky(symmetric)
    identity = jnp.eye(symmetric.shape[0], dtype=symmetric.dtype)
    return lax.linalg.triangular_solve(lower_factor, identity, left_side=True, lower=True)

def reference(front_slab, panels, diagonal_blocks, extend_maps):
    partner_plan = [(True, N_FC // 2), (True, 1), (False, N_FR // 2), (False, 1)]
    for level_index in range(LEVELS):
        grid_view = front_slab.reshape(N_FR, RD, N_FC, CD)
        top_rows = jnp.transpose(grid_view[:, :BLOCK], (0, 2, 1, 3))
        use_columns, flip_mask = partner_plan[level_index]
        if use_columns:
            partner_top = top_rows[:, np.arange(N_FC) ^ flip_mask]
        else:
            partner_top = top_rows[np.arange(N_FR) ^ flip_mask]
        row_map = jnp.broadcast_to(extend_maps[level_index][..., None], partner_top.shape)
        merged = top_rows + jnp.take_along_axis(partner_top, row_map, axis=2)
        grid_view = grid_view.at[:, :BLOCK].set(jnp.transpose(merged, (0, 2, 1, 3)))
        front_slab = grid_view.reshape(SLAB, NT)
        inverse = inverse_factor(diagonal_blocks[level_index])
        column_factor = jnp.dot(panels[level_index], inverse.T, precision=HIGHEST)
        front_slab = front_slab - jnp.dot(column_factor[:SLAB], column_factor.T, precision=HIGHEST)
    return front_slab
```

```python
import functools

import jax
import jax.numpy as jnp
from jax import lax
from jax.experimental import pallas as pl
from jax.experimental.pallas import tpu as pltpu
from jax.sharding import PartitionSpec as P

HIGHEST = lax.Precision.HIGHEST
MESH = pl.DeviceIdType.MESH
F32, BF16 = jnp.float32, jnp.bfloat16
PIVOT = 32
WIDTH = 256
LAG = 5


def split(x):
    high = x.astype(BF16)
    return high, (x - high.astype(F32)).astype(BF16)


def dot_t(a, b):
    return lax.dot_general(a, b, (((1,), (1,)), ((), ())), preferred_element_type=F32)


def product(a_high, a_low, b_high, b_low):
    return dot_t(a_high, b_high) + (dot_t(a_low, b_high) + dot_t(a_high, b_low))


def exact_dot(a, b):
    return jnp.dot(a, b, precision=HIGHEST, preferred_element_type=F32)


def small_inverse(m):
    size = m.shape[0]
    row = lax.broadcasted_iota(jnp.int32, m.shape, 0)
    lane = lax.broadcasted_iota(jnp.int32, m.shape, 1)
    for k in range(size):
        pivot = m[k : k + 1, k : k + 1]
        column = m[:, k : k + 1]
        pivot_row = jnp.where(lane[k : k + 1] == k, 1.0, m[k : k + 1]) / pivot
        m = jnp.where(row == k, pivot_row, jnp.where(lane == k, 0.0, m) - column * pivot_row)
    return m


def pivot_step(work):
    size = work.shape[0]
    w = work[...]
    inverse = small_inverse(w[:PIVOT, :PIVOT])
    lane = lax.broadcasted_iota(jnp.int32, (PIVOT, size), 1)
    sub = lax.broadcasted_iota(jnp.int32, (PIVOT, size), 0)
    top = jnp.where(lane < PIVOT, jnp.where(lane == sub, 1.0, 0.0), w[:PIVOT])
    top = exact_dot(inverse, top)
    below = w[PIVOT:]
    lane = lax.broadcasted_iota(jnp.int32, below.shape, 1)
    below = jnp.where(lane < PIVOT, 0.0, below) - exact_dot(below[:, :PIVOT], top)
    turn = lambda x: jnp.concatenate([x[:, PIVOT:], x[:, :PIVOT]], axis=1)
    work[pl.ds(0, size - PIVOT), :] = turn(below)
    work[pl.ds(size - PIVOT, PIVOT), :] = turn(top)


def kernel(
    n, nr, front_hbm, panels_hbm, diag_hbm, maps_ref, out_hbm,
    front, panels, gathered, work, shared, window, s_high, s_low, moves, received,
    diag_send, diag_recv, window_send, window_recv, window_load, inv_send, inv_recv,
    level_send, level_recv, load_sem, panel_sem, out_sem,
):
    c, r = lax.axis_index("fc"), lax.axis_index("fr")
    levels, pw = panels.shape[0], panels.shape[2]
    rows, cols = front.shape
    block = received.shape[1]
    chunks = cols // WIDTH
    groups = rows // block
    share = pw // n
    half = levels // 2
    even = c % 2 == 0

    barrier = pltpu.get_barrier_semaphore()
    for d in range(1, n):
        pl.semaphore_signal(barrier, inc=1, device_id={"fc": (c + d) % n}, device_id_type=MESH)
    for d in range(1, nr):
        pl.semaphore_signal(barrier, inc=1, device_id={"fr": (r + d) % nr}, device_id_type=MESH)
    own_window = []
    for g in range(groups):
        start = pl.multiple_of((r * rows) % cols + g * block, block)
        own_window.append(pltpu.make_async_copy(
            panels_hbm.at[:, pl.ds(start, block)], window.at[:, pl.ds(g * block, block)], window_load.at[g]
        ))
    front_load = pltpu.make_async_copy(front_hbm, front, load_sem.at[0])
    diag_rows = pl.ds(pl.multiple_of(c * share, 8), share)
    diag_load = pltpu.make_async_copy(diag_hbm, gathered.at[diag_rows], load_sem.at[1])
    diag_load.start()

    @pl.when(c == 0)
    def _():
        for copy in own_window:
            copy.start()

    pl.semaphore_wait(barrier, n - 1 + nr - 1)

    diag_copies = []
    for d in range(1, n):
        diag_copies.append(pltpu.make_async_remote_copy(
            src_ref=diag_hbm, dst_ref=gathered.at[diag_rows],
            send_sem=diag_send.at[d - 1], recv_sem=diag_recv.at[d - 1],
            device_id={"fc": (c + d) % n}, device_id_type=MESH,
        ))
    for copy in diag_copies:
        copy.start()

    def window_copy(g, h, way, target):
        part = window.at[pl.ds(h * half, half), pl.ds(g * block, block)]
        return pltpu.make_async_remote_copy(
            src_ref=part, dst_ref=part,
            send_sem=window_send.at[g, h, way], recv_sem=window_recv.at[g, h],
            device_id={"fc": target % n}, device_id_type=MESH,
        )

    def forwards(g, act):
        @pl.when(even)
        def _():
            act(window_copy(g, 0, 1, c + 1))

            @pl.when(c + 2 < n)
            def _():
                act(window_copy(g, 0, 0, c + 2))

        @pl.when(c == 0)
        def _():
            act(window_copy(g, 1, 0, 1 + c))

        @pl.when(jnp.logical_not(even))
        def _():
            @pl.when(c + 2 < n)
            def _():
                act(window_copy(g, 1, 0, c + 2))

            @pl.when(c >= 3)
            def _():
                act(window_copy(g, 1, 1, c - 1))

    def start(copy):
        copy.start()

    def wait_send(copy):
        copy.wait_send()

    def chain(g):
        @pl.when(c == 0)
        def _():
            own_window[g].wait()

        @pl.when(jnp.logical_and(c > 0, even))
        def _():
            window_copy(g, 0, 0, c + 1).wait_recv()

        @pl.when(jnp.logical_not(even))
        def _():
            window_copy(g, 1, 0, c + 1).wait_recv()

        forwards(g, start)

    def rest_of(g):
        @pl.when(jnp.logical_and(c > 0, even))
        def _():
            window_copy(g, 1, 0, c + 1).wait_recv()

        @pl.when(jnp.logical_not(even))
        def _():
            window_copy(g, 0, 0, c + 1).wait_recv()

    partners = [
        {"fc": (c + n // 2) % n},
        {"fc": c + 1 - 2 * (c % 2)},
        {"fr": (r + nr // 2) % nr},
        {"fr": r + 1 - 2 * (r % 2)},
    ]

    def columns(k):
        return pl.ds(pl.multiple_of(k * WIDTH, WIDTH), WIDTH)

    def level_copy(level, k):
        source = front_hbm if level == 0 else front
        return pltpu.make_async_remote_copy(
            src_ref=source.at[pl.ds(0, block), columns(k)],
            dst_ref=received.at[level, :, columns(k)],
            send_sem=level_send.at[level, k], recv_sem=level_recv.at[level, k],
            device_id=partners[level], device_id_type=MESH,
        )

    def panel_copy(k):
        part = pl.ds(pl.multiple_of(k * WIDTH, WIDTH), WIDTH)
        return pltpu.make_async_copy(panels_hbm.at[:, part], panels.at[:, part], panel_sem.at[k])

    def out_copy(k):
        return pltpu.make_async_copy(front.at[:, columns(k)], out_hbm.at[:, columns(k)], out_sem.at[k])

    @pl.when(c == 0)
    def _():
        chain(0)

    @pl.loop(0, chunks)
    def _(k):
        level_copy(0, k).start()

    @pl.when(c == 0)
    def _():
        for g in range(1, groups):
            chain(g)

    front_load.start()

    @pl.loop(0, chunks)
    def _(k):
        panel_copy(k).start()

    for level in range(levels):
        wanted = maps_ref[pl.ds(level, 1), :]
        index = lax.broadcasted_iota(jnp.int32, (block, block), 0)
        moves[level] = jnp.where(index == wanted, 1.0, 0.0).T.astype(BF16)

    diag_load.wait()
    for copy in diag_copies:
        copy.wait()
    transposed = gathered[...]
    symmetric = 0.5 * (transposed + transposed.T)
    sub = lax.broadcasted_iota(jnp.int32, symmetric.shape, 0)
    lane = lax.broadcasted_iota(jnp.int32, symmetric.shape, 1)
    diagonal = jnp.where(sub == lane, symmetric, 0.0)
    scale_row = lax.rsqrt(jnp.sum(diagonal, axis=0, keepdims=True))
    scale_column = lax.rsqrt(jnp.sum(diagonal, axis=1, keepdims=True))
    work[...] = symmetric * scale_row * scale_column
    shared[r, pl.ds(pw, 8), :] = jnp.broadcast_to(scale_row, (8, pw))

    @pl.loop(0, pw // PIVOT)
    def _(i):
        pivot_step(work)

        @pl.when(jnp.logical_and(c > 0, i == jnp.minimum(c // 2, pw // PIVOT - 1)))
        def _():
            chain(0)

    shared[r, pl.ds(0, pw), :] = work[...]
    inv_copies = []
    for d in range(1, nr):
        inv_copies.append(pltpu.make_async_remote_copy(
            src_ref=shared.at[r], dst_ref=shared.at[r],
            send_sem=inv_send.at[d - 1], recv_sem=inv_recv.at[d - 1],
            device_id={"fr": (r + d) % nr}, device_id_type=MESH,
        ))
    for copy in inv_copies:
        copy.start()
    rest_of(0)
    for copy in inv_copies:
        copy.wait()

    def scaled(x, level):
        return x * shared[level, pl.ds(pw, 1), :]

    def make_s(first, count):
        for level in range(levels):
            part = pl.ds(first, count)
            s = exact_dot(scaled(window[level, part, :], level), shared[level, pl.ds(0, pw), :])
            high, low = split(s)
            s_high[level, part, :] = high
            s_low[level, part, :] = low

    make_s(0, block)
    front_load.wait()

    def update(level, k, part):
        p_high, p_low = split(scaled(panels[level, columns(k), :], level))
        return product(s_high[level, part, :], s_low[level, part, :], p_high, p_low)

    def stage(level, k):
        if level == 0:
            panel_copy(k).wait()
        level_copy(level, k).wait()
        high, low = split(received[level, :, columns(k)])
        move = moves[level]
        moved = jnp.dot(move, high, preferred_element_type=F32) + jnp.dot(move, low, preferred_element_type=F32)
        top = front[pl.ds(0, block), columns(k)] + moved
        front[pl.ds(0, block), columns(k)] = top - update(level, k, pl.ds(0, block))
        if level + 1 < levels:
            level_copy(level + 1, k).start()

    @pl.loop(0, chunks + LAG)
    def _(t):
        for level in reversed(range(levels)):
            @pl.when(jnp.logical_and(t >= level, t < chunks + level))
            def _():
                stage(level, t - level)

        for g in range(1, groups):
            @pl.when(jnp.logical_and(c > 0, t == g - 1))
            def _():
                chain(g)

        @pl.when(t == LAG - 1)
        def _():
            for g in range(1, groups):
                rest_of(g)
                make_s(g * block, block)

        @pl.when(t >= LAG)
        def _():
            k = t - LAG
            part = pl.ds(block, rows - block)
            total = update(0, k, part)
            for level in range(1, levels):
                total = total + update(level, k, part)
            front[part, columns(k)] = front[part, columns(k)] - total
            out_copy(k).start()

    for g in range(groups):
        forwards(g, wait_send)

    @pl.loop(0, chunks)
    def _(k):
        out_copy(k).wait()


def body(front_slab, panels, diagonal_blocks, extend_maps):
    rows, cols = front_slab.shape
    levels, _, pw = panels.shape
    block = extend_maps.shape[3]
    n, nr = lax.axis_size("fc"), lax.axis_size("fr")
    chunks, groups = cols // WIDTH, rows // block
    mine = lax.dynamic_index_in_dim(diagonal_blocks, lax.axis_index("fr"), 0, keepdims=False).T
    anywhere = pl.BlockSpec(memory_space=pl.ANY)
    dma = pltpu.SemaphoreType.DMA
    return pl.pallas_call(
        functools.partial(kernel, n, nr),
        out_shape=jax.ShapeDtypeStruct((rows, cols), F32),
        in_specs=[anywhere, anywhere, anywhere, pl.BlockSpec(memory_space=pltpu.VMEM)],
        out_specs=anywhere,
        scratch_shapes=[
            pltpu.VMEM((rows, cols), F32),
            pltpu.VMEM(panels.shape, F32),
            pltpu.VMEM((pw, pw), F32),
            pltpu.VMEM((pw, pw), F32),
            pltpu.VMEM((levels, pw + 8, pw), F32),
            pltpu.VMEM((levels, rows, pw), F32),
            pltpu.VMEM((levels, rows, pw), BF16),
            pltpu.VMEM((levels, rows, pw), BF16),
            pltpu.VMEM((levels, block, block), BF16),
            pltpu.VMEM((levels, block, cols), F32),
            dma((n - 1,)),
            dma((n - 1,)),
            dma((groups, 2, 2)),
            dma((groups, 2)),
            dma((groups,)),
            dma((nr - 1,)),
            dma((nr - 1,)),
            dma((levels, chunks)),
            dma((levels, chunks)),
            dma((2,)),
            dma((chunks,)),
            dma((chunks,)),
        ],
        compiler_params=pltpu.CompilerParams(
            collective_id=0, has_side_effects=True, vmem_limit_bytes=50 * 2**20
        ),
        cost_estimate=pl.CostEstimate(
            flops=6 * rows * cols * levels * pw, bytes_accessed=8 * rows * cols + 4 * panels.size, transcendentals=0
        ),
    )(front_slab, panels, mine, extend_maps.reshape(levels, block))


def solution(mesh):
    in_specs = (P("fr", "fc"), P(None, "fc", None), P(None, None, "fc"), P(None, "fr", "fc", None))
    return jax.shard_map(body, mesh=mesh, in_specs=in_specs, out_specs=P("fr", "fc"), check_vma=False)
```

```python
import functools

import jax
import jax.numpy as jnp
from jax import lax
from jax.experimental import pallas as pl
from jax.experimental.pallas import tpu as pltpu
from jax.sharding import PartitionSpec as P

HIGHEST = lax.Precision.HIGHEST
MESH = pl.DeviceIdType.MESH
F32, BF16 = jnp.float32, jnp.bfloat16
PIVOT = 32
WIDTH = 256


def split(x):
    high = x.astype(BF16)
    return high, (x - high.astype(F32)).astype(BF16)


def dot_t(a, b):
    return lax.dot_general(a, b, (((1,), (1,)), ((), ())), preferred_element_type=F32)


def exact_dot(a, b):
    return jnp.dot(a, b, precision=HIGHEST, preferred_element_type=F32)


def small_inverse(m):
    size = m.shape[0]
    row = lax.broadcasted_iota(jnp.int32, m.shape, 0)
    lane = lax.broadcasted_iota(jnp.int32, m.shape, 1)
    for k in range(size):
        pivot = m[k : k + 1, k : k + 1]
        column = m[:, k : k + 1]
        pivot_row = jnp.where(lane[k : k + 1] == k, 1.0, m[k : k + 1]) / pivot
        m = jnp.where(row == k, pivot_row, jnp.where(lane == k, 0.0, m) - column * pivot_row)
    return m


def pivot_step(work):
    size = work.shape[0]
    w = work[...]
    inverse = small_inverse(w[:PIVOT, :PIVOT])
    lane = lax.broadcasted_iota(jnp.int32, (PIVOT, size), 1)
    sub = lax.broadcasted_iota(jnp.int32, (PIVOT, size), 0)
    top = jnp.where(lane < PIVOT, jnp.where(lane == sub, 1.0, 0.0), w[:PIVOT])
    top = exact_dot(inverse, top)
    below = w[PIVOT:]
    lane = lax.broadcasted_iota(jnp.int32, below.shape, 1)
    below = jnp.where(lane < PIVOT, 0.0, below) - exact_dot(below[:, :PIVOT], top)
    turn = lambda x: jnp.concatenate([x[:, PIVOT:], x[:, :PIVOT]], axis=1)
    work[pl.ds(0, size - PIVOT), :] = turn(below)
    work[pl.ds(size - PIVOT, PIVOT), :] = turn(top)


def kernel(
    n, nr, front_hbm, panels_hbm, diag_hbm, maps_ref, out_hbm,
    front, panels, gathered, work, shared, window, factors, moves, received,
    diag_send, diag_recv, window_send, window_recv, window_load, inv_send, inv_recv,
    level_send, level_recv, load_sem, panel_sem, out_sem,
):
    c, r = lax.axis_index("fc"), lax.axis_index("fr")
    levels, pw = panels.shape[0], panels.shape[2]
    rows, cols = front.shape
    block = received.shape[1]
    chunks = cols // WIDTH
    groups = rows // block
    share = pw // n
    half = levels // 2
    even = c % 2 == 0

    barrier = pltpu.get_barrier_semaphore()
    for d in range(1, n):
        pl.semaphore_signal(barrier, inc=1, device_id={"fc": (c + d) % n}, device_id_type=MESH)
    for d in range(1, nr):
        pl.semaphore_signal(barrier, inc=1, device_id={"fr": (r + d) % nr}, device_id_type=MESH)
    own_window = []
    for g in range(groups):
        start = pl.multiple_of((r * rows) % cols + g * block, block)
        own_window.append(pltpu.make_async_copy(
            panels_hbm.at[:, pl.ds(start, block)], window.at[:, pl.ds(g * block, block)], window_load.at[g]
        ))
    front_load = pltpu.make_async_copy(front_hbm, front, load_sem.at[0])
    diag_rows = pl.ds(pl.multiple_of(c * share, 8), share)
    diag_load = pltpu.make_async_copy(diag_hbm, gathered.at[diag_rows], load_sem.at[1])
    diag_load.start()

    @pl.when(c == 0)
    def _():
        for copy in own_window:
            copy.start()

    pl.semaphore_wait(barrier, n - 1 + nr - 1)

    diag_copies = []
    for d in range(1, n):
        diag_copies.append(pltpu.make_async_remote_copy(
            src_ref=diag_hbm, dst_ref=gathered.at[diag_rows],
            send_sem=diag_send.at[d - 1], recv_sem=diag_recv.at[d - 1],
            device_id={"fc": (c + d) % n}, device_id_type=MESH,
        ))
    for copy in diag_copies:
        copy.start()

    def window_copy(g, h, way, target):
        part = window.at[pl.ds(h * half, half), pl.ds(g * block, block)]
        return pltpu.make_async_remote_copy(
            src_ref=part, dst_ref=part,
            send_sem=window_send.at[g, h, way], recv_sem=window_recv.at[g, h],
            device_id={"fc": target % n}, device_id_type=MESH,
        )

    def across(g, act):
        @pl.when(even)
        def _():
            act(window_copy(g, 0, 1, c + 1))

    def forwards(g, act):
        @pl.when(even)
        def _():
            @pl.when(c + 2 < n)
            def _():
                act(window_copy(g, 0, 0, c + 2))

        @pl.when(c == 0)
        def _():
            act(window_copy(g, 1, 0, 1 + c))

        @pl.when(jnp.logical_not(even))
        def _():
            @pl.when(c + 2 < n)
            def _():
                act(window_copy(g, 1, 0, c + 2))

            @pl.when(c >= 3)
            def _():
                act(window_copy(g, 1, 1, c - 1))

    def start(copy):
        copy.start()

    def wait_send(copy):
        copy.wait_send()

    def chain(g):
        @pl.when(c == 0)
        def _():
            own_window[g].wait()

        @pl.when(jnp.logical_and(c > 0, even))
        def _():
            window_copy(g, 0, 0, c + 1).wait_recv()

        @pl.when(jnp.logical_not(even))
        def _():
            window_copy(g, 1, 0, c + 1).wait_recv()

        forwards(g, start)

        @pl.when(c > 0)
        def _():
            across(g, start)

    def rest_of(g):
        @pl.when(jnp.logical_and(c > 0, even))
        def _():
            window_copy(g, 1, 0, c + 1).wait_recv()

        @pl.when(jnp.logical_not(even))
        def _():
            window_copy(g, 0, 0, c + 1).wait_recv()

    partners = [
        {"fc": (c + n // 2) % n},
        {"fc": c + 1 - 2 * (c % 2)},
        {"fr": (r + nr // 2) % nr},
        {"fr": r + 1 - 2 * (r % 2)},
    ]

    def columns(k):
        return pl.ds(pl.multiple_of(k * WIDTH, WIDTH), WIDTH)

    def level_copy(level, k):
        source = front_hbm if level == 0 else front
        return pltpu.make_async_remote_copy(
            src_ref=source.at[pl.ds(0, block), columns(k)],
            dst_ref=received.at[level, :, columns(k)],
            send_sem=level_send.at[level, k], recv_sem=level_recv.at[level, k],
            device_id=partners[level], device_id_type=MESH,
        )

    def panel_copy(k):
        part = pl.ds(pl.multiple_of(k * WIDTH, WIDTH), WIDTH)
        return pltpu.make_async_copy(panels_hbm.at[:, part], panels.at[:, part], panel_sem.at[k])

    def out_copy(k):
        return pltpu.make_async_copy(front.at[:, columns(k)], out_hbm.at[:, columns(k)], out_sem.at[k])

    def start_first_level():
        @pl.loop(0, chunks)
        def _(k):
            level_copy(0, k).start()

    @pl.when(c == 0)
    def _():
        for g in range(groups):
            chain(g)

    passes_on = jnp.logical_and(c >= 2, c < n // 2)
    hop = jnp.minimum(c // 2, pw // PIVOT - groups)

    @pl.when(jnp.logical_not(passes_on))
    def _():
        start_first_level()

    front_load.start()

    @pl.loop(0, chunks)
    def _(k):
        panel_copy(k).start()

    for level in range(levels):
        wanted = maps_ref[pl.ds(level, 1), :]
        index = lax.broadcasted_iota(jnp.int32, (block, block), 0)
        move = jnp.where(index == wanted, 1.0, 0.0).T.astype(BF16)
        moves[level] = jnp.concatenate([move, move], axis=1)

    diag_load.wait()
    for copy in diag_copies:
        copy.wait()
    transposed = gathered[...]
    symmetric = 0.5 * (transposed + transposed.T)
    sub = lax.broadcasted_iota(jnp.int32, symmetric.shape, 0)
    lane = lax.broadcasted_iota(jnp.int32, symmetric.shape, 1)
    diagonal = jnp.where(sub == lane, symmetric, 0.0)
    scale_row = lax.rsqrt(jnp.sum(diagonal, axis=0, keepdims=True))
    scale_column = lax.rsqrt(jnp.sum(diagonal, axis=1, keepdims=True))
    work[...] = symmetric * scale_row * scale_column
    shared[r, pl.ds(pw, 8), :] = jnp.broadcast_to(scale_row, (8, pw))

    @pl.loop(0, pw // PIVOT)
    def _(i):
        pivot_step(work)

        for g in range(groups):
            @pl.when(jnp.logical_and(c > 0, i == hop + g))
            def _():
                chain(g)

                if g == groups - 1:
                    @pl.when(passes_on)
                    def _():
                        start_first_level()

            @pl.when(jnp.logical_and(c == 0, i == groups - 1))
            def _():
                across(g, start)

    shared[r, pl.ds(0, pw), :] = work[...]
    inv_copies = []
    for d in range(1, nr):
        inv_copies.append(pltpu.make_async_remote_copy(
            src_ref=shared.at[r], dst_ref=shared.at[r],
            send_sem=inv_send.at[d - 1], recv_sem=inv_recv.at[d - 1],
            device_id={"fr": (r + d) % nr}, device_id_type=MESH,
        ))
    for copy in inv_copies:
        copy.start()
    for g in range(groups):
        rest_of(g)
    for copy in inv_copies:
        copy.wait()

    def scaled(x, level):
        return x * shared[level, pl.ds(pw, 1), :]

    for level in range(levels):
        for g in range(groups):
            part = pl.ds(g * block, block)
            s = exact_dot(scaled(window[level, part, :], level), shared[level, pl.ds(0, pw), :])
            high, low = split(s)
            factors[level, part, :] = jnp.concatenate([high, low, high], axis=1)
    front_load.wait()

    def update(level, k):
        high, low = split(scaled(panels[level, columns(k), :], level))
        return dot_t(factors[level], jnp.concatenate([high, high, low], axis=1))

    def stage(level, k):
        if level == 0:
            panel_copy(k).wait()
        total = update(level, k)
        top, below = pl.ds(0, block), pl.ds(block, rows - block)
        level_copy(level, k).wait()
        pair = jnp.concatenate(split(received[level, :, columns(k)]), axis=0)
        moved = jnp.dot(moves[level], pair, preferred_element_type=F32)
        front[top, columns(k)] = front[top, columns(k)] + moved - total[:block]
        if level + 1 < levels:
            level_copy(level + 1, k).start()
        front[below, columns(k)] = front[below, columns(k)] - total[block:]
        if level + 1 == levels:
            out_copy(k).start()

    @pl.loop(0, chunks + levels - 1)
    def _(t):
        for level in reversed(range(levels)):
            @pl.when(jnp.logical_and(t >= level, t < chunks + level))
            def _():
                stage(level, t - level)

    for g in range(groups):
        forwards(g, wait_send)
        across(g, wait_send)

    @pl.loop(0, chunks)
    def _(k):
        out_copy(k).wait()


def body(front_slab, panels, diagonal_blocks, extend_maps):
    rows, cols = front_slab.shape
    levels, _, pw = panels.shape
    block = extend_maps.shape[3]
    n, nr = lax.axis_size("fc"), lax.axis_size("fr")
    chunks, groups = cols // WIDTH, rows // block
    mine = lax.dynamic_index_in_dim(diagonal_blocks, lax.axis_index("fr"), 0, keepdims=False).T
    anywhere = pl.BlockSpec(memory_space=pl.ANY)
    dma = pltpu.SemaphoreType.DMA
    return pl.pallas_call(
        functools.partial(kernel, n, nr),
        out_shape=jax.ShapeDtypeStruct((rows, cols), F32),
        in_specs=[anywhere, anywhere, anywhere, pl.BlockSpec(memory_space=pltpu.VMEM)],
        out_specs=anywhere,
        scratch_shapes=[
            pltpu.VMEM((rows, cols), F32),
            pltpu.VMEM(panels.shape, F32),
            pltpu.VMEM((pw, pw), F32),
            pltpu.VMEM((pw, pw), F32),
            pltpu.VMEM((levels, pw + 8, pw), F32),
            pltpu.VMEM((levels, rows, pw), F32),
            pltpu.VMEM((levels, rows, 3 * pw), BF16),
            pltpu.VMEM((levels, block, 2 * block), BF16),
            pltpu.VMEM((levels, block, cols), F32),
            dma((n - 1,)),
            dma((n - 1,)),
            dma((groups, 2, 2)),
            dma((groups, 2)),
            dma((groups,)),
            dma((nr - 1,)),
            dma((nr - 1,)),
            dma((levels, chunks)),
            dma((levels, chunks)),
            dma((2,)),
            dma((chunks,)),
            dma((chunks,)),
        ],
        compiler_params=pltpu.CompilerParams(
            collective_id=0, has_side_effects=True, vmem_limit_bytes=50 * 2**20
        ),
        cost_estimate=pl.CostEstimate(
            flops=6 * rows * cols * levels * pw, bytes_accessed=8 * rows * cols + 4 * panels.size, transcendentals=0
        ),
    )(front_slab, panels, mine, extend_maps.reshape(levels, block))


def solution(mesh):
    in_specs = (P("fr", "fc"), P(None, "fc", None), P(None, None, "fc"), P(None, "fr", "fc", None))
    return jax.shard_map(body, mesh=mesh, in_specs=in_specs, out_specs=P("fr", "fc"), check_vma=False)
```

```python
import functools

import jax
import jax.numpy as jnp
from jax import lax
from jax.experimental import pallas as pl
from jax.experimental.pallas import tpu as pltpu
from jax.sharding import PartitionSpec as P

HIGHEST = lax.Precision.HIGHEST
MESH = pl.DeviceIdType.MESH
F32, BF16 = jnp.float32, jnp.bfloat16
PIVOT = 32
WIDTH = 256


def split(x):
    high = x.astype(BF16)
    return high, (x - high.astype(F32)).astype(BF16)


def dot_t(a, b):
    return lax.dot_general(a, b, (((1,), (1,)), ((), ())), preferred_element_type=F32)


def exact_dot(a, b):
    return jnp.dot(a, b, precision=HIGHEST, preferred_element_type=F32)


def small_inverse(m):
    size, group = m.shape[0], 8
    shape = (group, size)
    sub = lax.broadcasted_iota(jnp.int32, shape, 0)
    lane = lax.broadcasted_iota(jnp.int32, shape, 1)
    parts = [m[i : i + group] for i in range(0, size, group)]

    def row_of(x, k):
        return jnp.broadcast_to(x[k : k + 1], shape)

    for q in range(size // group):
        spread = [
            [jnp.broadcast_to(part[:, q * group + j : q * group + j + 1], shape) for j in range(group)]
            for part in parts
        ]
        rows, columns = parts[q], list(spread[q])
        for k in range(group):
            at = q * group + k
            column = columns[k]
            scale = 1.0 / row_of(column, k)
            pivot_row = jnp.where(lane == at, scale, row_of(rows, k) * scale)
            rows = jnp.where(sub == k, pivot_row, jnp.where(lane == at, 0.0, rows) - column * pivot_row)
            for j in range(k + 1, group):
                other = row_of(columns[j], k) * scale
                columns[j] = jnp.where(sub == k, other, columns[j] - column * other)
        inside = jnp.logical_and(lane >= q * group, lane < (q + 1) * group)
        for i in range(len(parts)):
            if i != q:
                part = jnp.where(inside, 0.0, parts[i])
                for j in range(group):
                    part = part - spread[i][j] * row_of(rows, j)
                parts[i] = part
        parts[q] = rows
    return jnp.concatenate(parts, axis=0)


def pivot_step(work):
    size = work.shape[0]
    w = work[...]
    inverse = small_inverse(w[:PIVOT, :PIVOT])
    lane = lax.broadcasted_iota(jnp.int32, (PIVOT, size), 1)
    sub = lax.broadcasted_iota(jnp.int32, (PIVOT, size), 0)
    top = jnp.where(lane < PIVOT, jnp.where(lane == sub, 1.0, 0.0), w[:PIVOT])
    top = exact_dot(inverse, top)
    below = w[PIVOT:]
    lane = lax.broadcasted_iota(jnp.int32, below.shape, 1)
    below = jnp.where(lane < PIVOT, 0.0, below) - exact_dot(below[:, :PIVOT], top)
    turn = lambda x: jnp.concatenate([x[:, PIVOT:], x[:, :PIVOT]], axis=1)
    work[pl.ds(0, size - PIVOT), :] = turn(below)
    work[pl.ds(size - PIVOT, PIVOT), :] = turn(top)


def kernel(
    n, nr, front_hbm, panels_hbm, diag_hbm, maps_ref, out_hbm,
    front, panels, gathered, work, shared, window, factors, moves, received,
    diag_send, diag_recv, window_send, window_recv, window_load, inv_send, inv_recv,
    level_send, level_recv, load_sem, panel_sem, out_sem,
):
    c, r = lax.axis_index("fc"), lax.axis_index("fr")
    levels, pw = panels.shape[0], panels.shape[2]
    rows, cols = front.shape
    block = received.shape[1]
    chunks = cols // WIDTH
    groups = rows // block
    share = pw // n
    half = levels // 2
    even = c % 2 == 0

    barrier = pltpu.get_barrier_semaphore()
    for d in range(1, n):
        pl.semaphore_signal(barrier, inc=1, device_id={"fc": (c + d) % n}, device_id_type=MESH)
    for d in range(1, nr):
        pl.semaphore_signal(barrier, inc=1, device_id={"fr": (r + d) % nr}, device_id_type=MESH)
    own_window = []
    for g in range(groups):
        start = pl.multiple_of((r * rows) % cols + g * block, block)
        own_window.append(pltpu.make_async_copy(
            panels_hbm.at[:, pl.ds(start, block)], window.at[:, pl.ds(g * block, block)], window_load.at[g]
        ))
    front_load = pltpu.make_async_copy(front_hbm, front, load_sem.at[0])
    diag_rows = pl.ds(pl.multiple_of(c * share, 8), share)
    diag_load = pltpu.make_async_copy(diag_hbm, gathered.at[diag_rows], load_sem.at[1])
    diag_load.start()

    @pl.when(c == 0)
    def _():
        for copy in own_window:
            copy.start()

    pl.semaphore_wait(barrier, n - 1 + nr - 1)

    diag_copies = []
    for d in range(1, n):
        diag_copies.append(pltpu.make_async_remote_copy(
            src_ref=diag_hbm, dst_ref=gathered.at[diag_rows],
            send_sem=diag_send.at[d - 1], recv_sem=diag_recv.at[d - 1],
            device_id={"fc": (c + d) % n}, device_id_type=MESH,
        ))
    for copy in diag_copies:
        copy.start()

    def window_copy(g, h, way, target):
        part = window.at[pl.ds(h * half, half), pl.ds(g * block, block)]
        return pltpu.make_async_remote_copy(
            src_ref=part, dst_ref=part,
            send_sem=window_send.at[g, h, way], recv_sem=window_recv.at[g, h],
            device_id={"fc": target % n}, device_id_type=MESH,
        )

    def across(g, act):
        @pl.when(even)
        def _():
            act(window_copy(g, 0, 1, c + 1))

    def forwards(g, act):
        @pl.when(even)
        def _():
            @pl.when(c + 2 < n)
            def _():
                act(window_copy(g, 0, 0, c + 2))

        @pl.when(c == 0)
        def _():
            act(window_copy(g, 1, 0, 1 + c))

        @pl.when(jnp.logical_not(even))
        def _():
            @pl.when(c + 2 < n)
            def _():
                act(window_copy(g, 1, 0, c + 2))

            @pl.when(c >= 3)
            def _():
                act(window_copy(g, 1, 1, c - 1))

    def start(copy):
        copy.start()

    def wait_send(copy):
        copy.wait_send()

    def chain(g):
        @pl.when(c == 0)
        def _():
            own_window[g].wait()

        @pl.when(jnp.logical_and(c > 0, even))
        def _():
            window_copy(g, 0, 0, c + 1).wait_recv()

        @pl.when(jnp.logical_not(even))
        def _():
            window_copy(g, 1, 0, c + 1).wait_recv()

        forwards(g, start)

        @pl.when(c > 0)
        def _():
            across(g, start)

    def rest_of(g):
        @pl.when(jnp.logical_and(c > 0, even))
        def _():
            window_copy(g, 1, 0, c + 1).wait_recv()

        @pl.when(jnp.logical_not(even))
        def _():
            window_copy(g, 0, 0, c + 1).wait_recv()

    partners = [
        {"fc": (c + n // 2) % n},
        {"fc": c + 1 - 2 * (c % 2)},
        {"fr": (r + nr // 2) % nr},
        {"fr": r + 1 - 2 * (r % 2)},
    ]

    def columns(k):
        return pl.ds(pl.multiple_of(k * WIDTH, WIDTH), WIDTH)

    def level_copy(level, k):
        source = front_hbm if level == 0 else front
        return pltpu.make_async_remote_copy(
            src_ref=source.at[pl.ds(0, block), columns(k)],
            dst_ref=received.at[level, :, columns(k)],
            send_sem=level_send.at[level, k], recv_sem=level_recv.at[level, k],
            device_id=partners[level], device_id_type=MESH,
        )

    def panel_copy(k):
        part = pl.ds(pl.multiple_of(k * WIDTH, WIDTH), WIDTH)
        return pltpu.make_async_copy(panels_hbm.at[:, part], panels.at[:, part], panel_sem.at[k])

    def out_copy(k):
        return pltpu.make_async_copy(front.at[:, columns(k)], out_hbm.at[:, columns(k)], out_sem.at[k])

    def start_first_level():
        @pl.loop(0, chunks)
        def _(k):
            level_copy(0, k).start()

    @pl.when(c == 0)
    def _():
        for g in range(groups):
            chain(g)

    passes_on = jnp.logical_and(c >= 2, c < n // 2)
    hop = jnp.minimum(c // 2, pw // PIVOT - groups)

    @pl.when(jnp.logical_not(passes_on))
    def _():
        start_first_level()

    front_load.start()

    @pl.loop(0, chunks)
    def _(k):
        panel_copy(k).start()

    for level in range(levels):
        wanted = maps_ref[pl.ds(level, 1), :]
        index = lax.broadcasted_iota(jnp.int32, (block, block), 0)
        move = jnp.where(index == wanted, 1.0, 0.0).T.astype(BF16)
        moves[level] = jnp.concatenate([move, move], axis=1)

    diag_load.wait()
    for copy in diag_copies:
        copy.wait()
    transposed = gathered[...]
    symmetric = 0.5 * (transposed + transposed.T)
    sub = lax.broadcasted_iota(jnp.int32, symmetric.shape, 0)
    lane = lax.broadcasted_iota(jnp.int32, symmetric.shape, 1)
    diagonal = jnp.where(sub == lane, symmetric, 0.0)
    scale_row = lax.rsqrt(jnp.sum(diagonal, axis=0, keepdims=True))
    scale_column = lax.rsqrt(jnp.sum(diagonal, axis=1, keepdims=True))
    work[...] = symmetric * scale_row * scale_column
    shared[r, pl.ds(pw, 8), :] = jnp.broadcast_to(scale_row, (8, pw))

    @pl.loop(0, pw // PIVOT)
    def _(i):
        pivot_step(work)

        for g in range(groups):
            @pl.when(jnp.logical_and(c > 0, i == hop + g))
            def _():
                chain(g)

                if g == groups - 1:
                    @pl.when(passes_on)
                    def _():
                        start_first_level()

            @pl.when(jnp.logical_and(c == 0, i == groups - 1))
            def _():
                across(g, start)

    shared[r, pl.ds(0, pw), :] = work[...]
    inv_copies = []
    for d in range(1, nr):
        inv_copies.append(pltpu.make_async_remote_copy(
            src_ref=shared.at[r], dst_ref=shared.at[r],
            send_sem=inv_send.at[d - 1], recv_sem=inv_recv.at[d - 1],
            device_id={"fr": (r + d) % nr}, device_id_type=MESH,
        ))
    for copy in inv_copies:
        copy.start()
    for g in range(groups):
        rest_of(g)
    for copy in inv_copies:
        copy.wait()

    def scaled(x, level):
        return x * shared[level, pl.ds(pw, 1), :]

    for level in range(levels):
        for g in range(groups):
            part = pl.ds(g * block, block)
            s = exact_dot(scaled(window[level, part, :], level), shared[level, pl.ds(0, pw), :])
            high, low = split(s)
            factors[level, part, :] = jnp.concatenate([high, low, high], axis=1)
    front_load.wait()

    def update(level, k):
        high, low = split(scaled(panels[level, columns(k), :], level))
        return dot_t(factors[level], jnp.concatenate([high, high, low], axis=1))

    def stage(level, k):
        if level == 0:
            panel_copy(k).wait()
        total = update(level, k)
        top, below = pl.ds(0, block), pl.ds(block, rows - block)
        level_copy(level, k).wait()
        pair = jnp.concatenate(split(received[level, :, columns(k)]), axis=0)
        moved = jnp.dot(moves[level], pair, preferred_element_type=F32)
        front[top, columns(k)] = front[top, columns(k)] + moved - total[:block]
        if level + 1 < levels:
            level_copy(level + 1, k).start()
        front[below, columns(k)] = front[below, columns(k)] - total[block:]
        if level + 1 == levels:
            out_copy(k).start()

    @pl.loop(0, chunks + levels - 1)
    def _(t):
        for level in reversed(range(levels)):
            @pl.when(jnp.logical_and(t >= level, t < chunks + level))
            def _():
                stage(level, t - level)

    for g in range(groups):
        forwards(g, wait_send)
        across(g, wait_send)

    @pl.loop(0, chunks)
    def _(k):
        out_copy(k).wait()


def body(front_slab, panels, diagonal_blocks, extend_maps):
    rows, cols = front_slab.shape
    levels, _, pw = panels.shape
    block = extend_maps.shape[3]
    n, nr = lax.axis_size("fc"), lax.axis_size("fr")
    chunks, groups = cols // WIDTH, rows // block
    mine = lax.dynamic_index_in_dim(diagonal_blocks, lax.axis_index("fr"), 0, keepdims=False).T
    anywhere = pl.BlockSpec(memory_space=pl.ANY)
    dma = pltpu.SemaphoreType.DMA
    return pl.pallas_call(
        functools.partial(kernel, n, nr),
        out_shape=jax.ShapeDtypeStruct((rows, cols), F32),
        in_specs=[anywhere, anywhere, anywhere, pl.BlockSpec(memory_space=pltpu.VMEM)],
        out_specs=anywhere,
        scratch_shapes=[
            pltpu.VMEM((rows, cols), F32),
            pltpu.VMEM(panels.shape, F32),
            pltpu.VMEM((pw, pw), F32),
            pltpu.VMEM((pw, pw), F32),
            pltpu.VMEM((levels, pw + 8, pw), F32),
            pltpu.VMEM((levels, rows, pw), F32),
            pltpu.VMEM((levels, rows, 3 * pw), BF16),
            pltpu.VMEM((levels, block, 2 * block), BF16),
            pltpu.VMEM((levels, block, cols), F32),
            dma((n - 1,)),
            dma((n - 1,)),
            dma((groups, 2, 2)),
            dma((groups, 2)),
            dma((groups,)),
            dma((nr - 1,)),
            dma((nr - 1,)),
            dma((levels, chunks)),
            dma((levels, chunks)),
            dma((2,)),
            dma((chunks,)),
            dma((chunks,)),
        ],
        compiler_params=pltpu.CompilerParams(
            collective_id=0, has_side_effects=True, vmem_limit_bytes=50 * 2**20
        ),
        cost_estimate=pl.CostEstimate(
            flops=6 * rows * cols * levels * pw, bytes_accessed=8 * rows * cols + 4 * panels.size, transcendentals=0
        ),
    )(front_slab, panels, mine, extend_maps.reshape(levels, block))


def solution(mesh):
    in_specs = (P("fr", "fc"), P(None, "fc", None), P(None, None, "fc"), P(None, "fr", "fc", None))
    return jax.shard_map(body, mesh=mesh, in_specs=in_specs, out_specs=P("fr", "fc"), check_vma=False)
```

```python
import functools

import jax
import jax.numpy as jnp
from jax import lax
from jax.experimental import pallas as pl
from jax.experimental.pallas import tpu as pltpu
from jax.sharding import PartitionSpec as P

HIGHEST = lax.Precision.HIGHEST
MESH = pl.DeviceIdType.MESH
F32, BF16 = jnp.float32, jnp.bfloat16
PIVOT = 32
WIDTH = 256
SKEW = 2
EARLY = 2


def split(x):
    high = x.astype(BF16)
    return high, (x - high.astype(F32)).astype(BF16)


def dot_t(a, b):
    return lax.dot_general(a, b, (((1,), (1,)), ((), ())), preferred_element_type=F32)


def exact_dot(a, b):
    return jnp.dot(a, b, precision=HIGHEST, preferred_element_type=F32)


def small_inverse(m):
    size, group = m.shape[0], 8
    shape = (group, size)
    sub = lax.broadcasted_iota(jnp.int32, shape, 0)
    lane = lax.broadcasted_iota(jnp.int32, shape, 1)
    parts = [m[i : i + group] for i in range(0, size, group)]

    def row_of(x, k):
        return jnp.broadcast_to(x[k : k + 1], shape)

    for q in range(size // group):
        spread = [
            [jnp.broadcast_to(part[:, q * group + j : q * group + j + 1], shape) for j in range(group)]
            for part in parts
        ]
        rows, columns = parts[q], list(spread[q])
        for k in range(group):
            at = q * group + k
            column = columns[k]
            scale = 1.0 / row_of(column, k)
            pivot_row = jnp.where(lane == at, scale, row_of(rows, k) * scale)
            rows = jnp.where(sub == k, pivot_row, jnp.where(lane == at, 0.0, rows) - column * pivot_row)
            for j in range(k + 1, group):
                other = row_of(columns[j], k) * scale
                columns[j] = jnp.where(sub == k, other, columns[j] - column * other)
        inside = jnp.logical_and(lane >= q * group, lane < (q + 1) * group)
        for i in range(len(parts)):
            if i != q:
                part = jnp.where(inside, 0.0, parts[i])
                for j in range(group):
                    part = part - spread[i][j] * row_of(rows, j)
                parts[i] = part
        parts[q] = rows
    return jnp.concatenate(parts, axis=0)


def pivot_step(work):
    size = work.shape[0]
    w = work[...]
    inverse = small_inverse(w[:PIVOT, :PIVOT])
    lane = lax.broadcasted_iota(jnp.int32, (PIVOT, size), 1)
    sub = lax.broadcasted_iota(jnp.int32, (PIVOT, size), 0)
    top = jnp.where(lane < PIVOT, jnp.where(lane == sub, 1.0, 0.0), w[:PIVOT])
    top = exact_dot(inverse, top)
    below = w[PIVOT:]
    lane = lax.broadcasted_iota(jnp.int32, below.shape, 1)
    below = jnp.where(lane < PIVOT, 0.0, below) - exact_dot(below[:, :PIVOT], top)
    turn = lambda x: jnp.concatenate([x[:, PIVOT:], x[:, :PIVOT]], axis=1)
    work[pl.ds(0, size - PIVOT), :] = turn(below)
    work[pl.ds(size - PIVOT, PIVOT), :] = turn(top)


def kernel(
    n, nr, front_hbm, panels_hbm, diag_hbm, maps_ref, out_hbm,
    front, panels, gathered, work, shared, window, factors, moves, received,
    diag_send, diag_recv, window_send, window_recv, window_load, inv_send, inv_recv,
    level_send, level_recv, load_sem, panel_sem, out_sem,
):
    c, r = lax.axis_index("fc"), lax.axis_index("fr")
    levels, pw = panels.shape[0], panels.shape[2]
    rows, cols = front.shape
    block = received.shape[1]
    chunks = cols // WIDTH
    groups = rows // block
    share = pw // n
    half = levels // 2
    even = c % 2 == 0

    barrier = pltpu.get_barrier_semaphore()
    for d in range(1, n):
        pl.semaphore_signal(barrier, inc=1, device_id={"fc": (c + d) % n}, device_id_type=MESH)
    for d in range(1, nr):
        pl.semaphore_signal(barrier, inc=1, device_id={"fr": (r + d) % nr}, device_id_type=MESH)
    own_window = []
    for g in range(groups):
        start = pl.multiple_of((r * rows) % cols + g * block, block)
        own_window.append(pltpu.make_async_copy(
            panels_hbm.at[:, pl.ds(start, block)], window.at[:, pl.ds(g * block, block)], window_load.at[g]
        ))
    front_load = pltpu.make_async_copy(front_hbm, front, load_sem.at[0])
    diag_rows = pl.ds(pl.multiple_of(c * share, 8), share)
    diag_load = pltpu.make_async_copy(diag_hbm, gathered.at[diag_rows], load_sem.at[1])
    diag_load.start()

    @pl.when(c == 0)
    def _():
        for copy in own_window:
            copy.start()

    pl.semaphore_wait(barrier, n - 1 + nr - 1)

    diag_copies = []
    for d in range(1, n):
        diag_copies.append(pltpu.make_async_remote_copy(
            src_ref=diag_hbm, dst_ref=gathered.at[diag_rows],
            send_sem=diag_send.at[d - 1], recv_sem=diag_recv.at[d - 1],
            device_id={"fc": (c + d) % n}, device_id_type=MESH,
        ))
    for copy in diag_copies:
        copy.start()

    def window_copy(g, h, way, target):
        part = window.at[pl.ds(h * half, half), pl.ds(g * block, block)]
        return pltpu.make_async_remote_copy(
            src_ref=part, dst_ref=part,
            send_sem=window_send.at[g, h, way], recv_sem=window_recv.at[g, h],
            device_id={"fc": target % n}, device_id_type=MESH,
        )

    def across(g, act):
        @pl.when(even)
        def _():
            act(window_copy(g, 0, 1, c + 1))

    def forwards(g, act):
        @pl.when(even)
        def _():
            @pl.when(c + 2 < n)
            def _():
                act(window_copy(g, 0, 0, c + 2))

        @pl.when(c == 0)
        def _():
            act(window_copy(g, 1, 0, 1 + c))

        @pl.when(jnp.logical_not(even))
        def _():
            @pl.when(c + 2 < n)
            def _():
                act(window_copy(g, 1, 0, c + 2))

            @pl.when(c >= 3)
            def _():
                act(window_copy(g, 1, 1, c - 1))

    def start(copy):
        copy.start()

    def wait_send(copy):
        copy.wait_send()

    def chain(g):
        @pl.when(c == 0)
        def _():
            own_window[g].wait()

        @pl.when(jnp.logical_and(c > 0, even))
        def _():
            window_copy(g, 0, 0, c + 1).wait_recv()

        @pl.when(jnp.logical_not(even))
        def _():
            window_copy(g, 1, 0, c + 1).wait_recv()

        forwards(g, start)

        @pl.when(c > 0)
        def _():
            across(g, start)

    def rest_of(g):
        @pl.when(jnp.logical_and(c > 0, even))
        def _():
            window_copy(g, 1, 0, c + 1).wait_recv()

        @pl.when(jnp.logical_not(even))
        def _():
            window_copy(g, 0, 0, c + 1).wait_recv()

    partners = [
        {"fc": (c + n // 2) % n},
        {"fc": c + 1 - 2 * (c % 2)},
        {"fr": (r + nr // 2) % nr},
        {"fr": r + 1 - 2 * (r % 2)},
    ]

    def columns(k):
        return pl.ds(pl.multiple_of(k * WIDTH, WIDTH), WIDTH)

    def level_copy(level, k):
        source = front_hbm if level == 0 else front
        return pltpu.make_async_remote_copy(
            src_ref=source.at[pl.ds(0, block), columns(k)],
            dst_ref=received.at[level, :, columns(k)],
            send_sem=level_send.at[level, k], recv_sem=level_recv.at[level, k],
            device_id=partners[level], device_id_type=MESH,
        )

    def panel_copy(k):
        part = pl.ds(pl.multiple_of(k * WIDTH, WIDTH), WIDTH)
        return pltpu.make_async_copy(panels_hbm.at[:, part], panels.at[:, part], panel_sem.at[k])

    def out_copy(k):
        return pltpu.make_async_copy(front.at[:, columns(k)], out_hbm.at[:, columns(k)], out_sem.at[k])

    def start_first_level(first, end):
        @pl.loop(first, end)
        def _(k):
            level_copy(0, k).start()

    @pl.when(c == 0)
    def _():
        for g in range(groups):
            chain(g)

    upper = c >= n // 2
    hop = jnp.minimum(c // 2 - 1, pw // PIVOT - groups)

    @pl.when(c >= 2)
    def _():
        start_first_level(0, EARLY)

    @pl.when(upper)
    def _():
        start_first_level(EARLY, chunks)

    front_load.start()

    @pl.loop(0, chunks)
    def _(k):
        panel_copy(k).start()

    for level in range(levels):
        wanted = maps_ref[pl.ds(level, 1), :]
        index = lax.broadcasted_iota(jnp.int32, (block, block), 0)
        move = jnp.where(index == wanted, 1.0, 0.0).T.astype(BF16)
        moves[level] = jnp.concatenate([move, move], axis=1)

    diag_load.wait()
    for copy in diag_copies:
        copy.wait()
    transposed = gathered[...]
    symmetric = 0.5 * (transposed + transposed.T)
    sub = lax.broadcasted_iota(jnp.int32, symmetric.shape, 0)
    lane = lax.broadcasted_iota(jnp.int32, symmetric.shape, 1)
    diagonal = jnp.where(sub == lane, symmetric, 0.0)
    scale_row = lax.rsqrt(jnp.sum(diagonal, axis=0, keepdims=True))
    scale_column = lax.rsqrt(jnp.sum(diagonal, axis=1, keepdims=True))
    work[...] = symmetric * scale_row * scale_column
    shared[r, pl.ds(pw, 8), :] = jnp.broadcast_to(scale_row, (8, pw))

    @pl.loop(0, pw // PIVOT)
    def _(i):
        pivot_step(work)

        for g in range(groups):
            @pl.when(jnp.logical_and(c > 0, i == jnp.maximum(hop + g, 0)))
            def _():
                chain(g)

            @pl.when(jnp.logical_and(c == 0, i == groups - 1))
            def _():
                across(g, start)

        @pl.when(jnp.logical_and(c < 2, i == groups - 1))
        def _():
            start_first_level(0, EARLY)

        @pl.when(jnp.logical_and(jnp.logical_not(upper), i == jnp.maximum(hop, 0) + groups - 1))
        def _():
            start_first_level(EARLY, chunks)

    shared[r, pl.ds(0, pw), :] = work[...]
    def inv_copy(index, slot, target):
        return pltpu.make_async_remote_copy(
            src_ref=shared.at[slot], dst_ref=shared.at[slot],
            send_sem=inv_send.at[index], recv_sem=inv_recv.at[index],
            device_id=target, device_id_type=MESH,
        )

    far, near = partners[2], partners[3]
    far_copy = inv_copy(0, r, far)
    near_copy = inv_copy(1, r, near)
    pass_copy = inv_copy(2, far["fr"], near)
    far_copy.start()
    near_copy.start()
    far_copy.wait_recv()
    pass_copy.start()
    for g in range(groups):
        rest_of(g)
    far_copy.wait_send()
    near_copy.wait()
    pass_copy.wait()

    def scaled(x, level):
        return x * shared[level, pl.ds(pw, 1), :]

    for level in range(levels):
        x_high, x_low = split(scaled(window[level], level))
        high, low = split(shared[level, pl.ds(0, pw), :])
        s = jnp.dot(
            jnp.concatenate([x_high, x_low, x_high], axis=1),
            jnp.concatenate([high, high, low], axis=0),
            preferred_element_type=F32,
        )
        high, low = split(s)
        factors[level] = jnp.concatenate([high, low, high], axis=1)
    front_load.wait()

    def update(level, k):
        high, low = split(scaled(panels[level, columns(k), :], level))
        return dot_t(factors[level], jnp.concatenate([high, high, low], axis=1))

    def stage(level, k):
        if level == 0:
            panel_copy(k).wait()
        total = update(level, k)
        top, below = pl.ds(0, block), pl.ds(block, rows - block)
        level_copy(level, k).wait()
        pair = jnp.concatenate(split(received[level, :, columns(k)]), axis=0)
        moved = jnp.dot(moves[level], pair, preferred_element_type=F32)
        front[top, columns(k)] = front[top, columns(k)] + moved - total[:block]
        if level + 1 < levels:
            level_copy(level + 1, k).start()
        front[below, columns(k)] = front[below, columns(k)] - total[block:]
        if level + 1 == levels:
            out_copy(k).start()

    @pl.loop(0, chunks + SKEW * (levels - 1))
    def _(t):
        for level in reversed(range(levels)):
            @pl.when(jnp.logical_and(t >= SKEW * level, t < chunks + SKEW * level))
            def _():
                stage(level, t - SKEW * level)

    for g in range(groups):
        forwards(g, wait_send)
        across(g, wait_send)

    @pl.loop(0, chunks)
    def _(k):
        out_copy(k).wait()


def body(front_slab, panels, diagonal_blocks, extend_maps):
    rows, cols = front_slab.shape
    levels, _, pw = panels.shape
    block = extend_maps.shape[3]
    n, nr = lax.axis_size("fc"), lax.axis_size("fr")
    chunks, groups = cols // WIDTH, rows // block
    mine = lax.dynamic_index_in_dim(diagonal_blocks, lax.axis_index("fr"), 0, keepdims=False).T
    anywhere = pl.BlockSpec(memory_space=pl.ANY)
    dma = pltpu.SemaphoreType.DMA
    return pl.pallas_call(
        functools.partial(kernel, n, nr),
        out_shape=jax.ShapeDtypeStruct((rows, cols), F32),
        in_specs=[anywhere, anywhere, anywhere, pl.BlockSpec(memory_space=pltpu.VMEM)],
        out_specs=anywhere,
        scratch_shapes=[
            pltpu.VMEM((rows, cols), F32),
            pltpu.VMEM(panels.shape, F32),
            pltpu.VMEM((pw, pw), F32),
            pltpu.VMEM((pw, pw), F32),
            pltpu.VMEM((levels, pw + 8, pw), F32),
            pltpu.VMEM((levels, rows, pw), F32),
            pltpu.VMEM((levels, rows, 3 * pw), BF16),
            pltpu.VMEM((levels, block, 2 * block), BF16),
            pltpu.VMEM((levels, block, cols), F32),
            dma((n - 1,)),
            dma((n - 1,)),
            dma((groups, 2, 2)),
            dma((groups, 2)),
            dma((groups,)),
            dma((nr - 1,)),
            dma((nr - 1,)),
            dma((levels, chunks)),
            dma((levels, chunks)),
            dma((2,)),
            dma((chunks,)),
            dma((chunks,)),
        ],
        compiler_params=pltpu.CompilerParams(
            collective_id=0, has_side_effects=True, vmem_limit_bytes=50 * 2**20
        ),
        cost_estimate=pl.CostEstimate(
            flops=6 * rows * cols * levels * pw, bytes_accessed=8 * rows * cols + 4 * panels.size, transcendentals=0
        ),
    )(front_slab, panels, mine, extend_maps.reshape(levels, block))


def solution(mesh):
    in_specs = (P("fr", "fc"), P(None, "fc", None), P(None, None, "fc"), P(None, "fr", "fc", None))
    return jax.shard_map(body, mesh=mesh, in_specs=in_specs, out_specs=P("fr", "fc"), check_vma=False)
```

```python
import functools

import jax
import jax.numpy as jnp
from jax import lax
from jax.experimental import pallas as pl
from jax.experimental.pallas import tpu as pltpu
from jax.sharding import PartitionSpec as P

HIGHEST = lax.Precision.HIGHEST
MESH = pl.DeviceIdType.MESH
F32, BF16 = jnp.float32, jnp.bfloat16
PIVOT = 32
WIDTH = 256
SKEW = 2
EARLY = 2


def split(x):
    high = x.astype(BF16)
    return high, (x - high.astype(F32)).astype(BF16)


def dot_t(a, b):
    return lax.dot_general(a, b, (((1,), (1,)), ((), ())), preferred_element_type=F32)


def exact_dot(a, b):
    return jnp.dot(a, b, precision=HIGHEST, preferred_element_type=F32)


def small_inverse(m):
    size, group = m.shape[0], 8
    shape = (group, size)
    sub = lax.broadcasted_iota(jnp.int32, shape, 0)
    lane = lax.broadcasted_iota(jnp.int32, shape, 1)
    parts = [m[i : i + group] for i in range(0, size, group)]

    def row_of(x, k):
        return jnp.broadcast_to(x[k : k + 1], shape)

    for q in range(size // group):
        spread = [
            [jnp.broadcast_to(part[:, q * group + j : q * group + j + 1], shape) for j in range(group)]
            for part in parts
        ]
        rows, columns = parts[q], list(spread[q])
        for k in range(group):
            at = q * group + k
            column = columns[k]
            scale = 1.0 / row_of(column, k)
            pivot_row = jnp.where(lane == at, scale, row_of(rows, k) * scale)
            rows = jnp.where(sub == k, pivot_row, jnp.where(lane == at, 0.0, rows) - column * pivot_row)
            for j in range(k + 1, group):
                other = row_of(columns[j], k) * scale
                columns[j] = jnp.where(sub == k, other, columns[j] - column * other)
        inside = jnp.logical_and(lane >= q * group, lane < (q + 1) * group)
        for i in range(len(parts)):
            if i != q:
                part = jnp.where(inside, 0.0, parts[i])
                for j in range(group):
                    part = part - spread[i][j] * row_of(rows, j)
                parts[i] = part
        parts[q] = rows
    return jnp.concatenate(parts, axis=0)


def pivot_step(work):
    size = work.shape[0]
    w = work[...]
    inverse = small_inverse(w[:PIVOT, :PIVOT])
    lane = lax.broadcasted_iota(jnp.int32, (PIVOT, size), 1)
    sub = lax.broadcasted_iota(jnp.int32, (PIVOT, size), 0)
    top = jnp.where(lane < PIVOT, jnp.where(lane == sub, 1.0, 0.0), w[:PIVOT])
    top = exact_dot(inverse, top)
    below = w[PIVOT:]
    lane = lax.broadcasted_iota(jnp.int32, below.shape, 1)
    below = jnp.where(lane < PIVOT, 0.0, below) - exact_dot(below[:, :PIVOT], top)
    turn = lambda x: jnp.concatenate([x[:, PIVOT:], x[:, :PIVOT]], axis=1)
    work[pl.ds(0, size - PIVOT), :] = turn(below)
    work[pl.ds(size - PIVOT, PIVOT), :] = turn(top)


def kernel(
    n, nr, front_hbm, panels_hbm, diag_hbm, maps_ref, out_hbm,
    front, panels, gathered, work, shared, window, factors, moves, received,
    diag_send, diag_recv, window_send, window_recv, window_load, inv_send, inv_recv,
    level_send, level_recv, load_sem, panel_sem, out_sem,
):
    c, r = lax.axis_index("fc"), lax.axis_index("fr")
    levels, pw = panels.shape[0], panels.shape[2]
    rows, cols = front.shape
    block = received.shape[1]
    chunks = cols // WIDTH
    groups = rows // block
    share = pw // n
    half = levels // 2
    even = c % 2 == 0

    barrier = pltpu.get_barrier_semaphore()
    for d in range(1, n):
        pl.semaphore_signal(barrier, inc=1, device_id={"fc": (c + d) % n}, device_id_type=MESH)
    for d in range(1, nr):
        pl.semaphore_signal(barrier, inc=1, device_id={"fr": (r + d) % nr}, device_id_type=MESH)
    own_window = []
    for g in range(groups):
        start = pl.multiple_of((r * rows) % cols + g * block, block)
        own_window.append(pltpu.make_async_copy(
            panels_hbm.at[:, pl.ds(start, block)], window.at[:, pl.ds(g * block, block)], window_load.at[g]
        ))
    front_load = pltpu.make_async_copy(front_hbm, front, load_sem.at[0])
    diag_rows = pl.ds(pl.multiple_of(c * share, 8), share)
    diag_load = pltpu.make_async_copy(diag_hbm, gathered.at[diag_rows], load_sem.at[1])
    diag_load.start()

    @pl.when(c == 0)
    def _():
        for copy in own_window:
            copy.start()

    pl.semaphore_wait(barrier, n - 1 + nr - 1)

    diag_copies = []
    for d in range(1, n):
        diag_copies.append(pltpu.make_async_remote_copy(
            src_ref=diag_hbm, dst_ref=gathered.at[diag_rows],
            send_sem=diag_send.at[d - 1], recv_sem=diag_recv.at[d - 1],
            device_id={"fc": (c + d) % n}, device_id_type=MESH,
        ))
    for copy in diag_copies:
        copy.start()

    def window_copy(g, h, way, target):
        part = window.at[pl.ds(h * half, half), pl.ds(g * block, block)]
        return pltpu.make_async_remote_copy(
            src_ref=part, dst_ref=part,
            send_sem=window_send.at[g, h, way], recv_sem=window_recv.at[g, h],
            device_id={"fc": target % n}, device_id_type=MESH,
        )

    def across(g, act):
        @pl.when(even)
        def _():
            act(window_copy(g, 0, 1, c + 1))

    def forwards(g, act):
        @pl.when(even)
        def _():
            @pl.when(c + 2 < n)
            def _():
                act(window_copy(g, 0, 0, c + 2))

        @pl.when(c == 0)
        def _():
            act(window_copy(g, 1, 0, 1 + c))

        @pl.when(jnp.logical_not(even))
        def _():
            @pl.when(c + 2 < n)
            def _():
                act(window_copy(g, 1, 0, c + 2))

            @pl.when(c >= 3)
            def _():
                act(window_copy(g, 1, 1, c - 1))

    def start(copy):
        copy.start()

    def wait_send(copy):
        copy.wait_send()

    def chain(g):
        @pl.when(c == 0)
        def _():
            own_window[g].wait()

        @pl.when(jnp.logical_and(c > 0, even))
        def _():
            window_copy(g, 0, 0, c + 1).wait_recv()

        @pl.when(jnp.logical_not(even))
        def _():
            window_copy(g, 1, 0, c + 1).wait_recv()

        forwards(g, start)

        @pl.when(c > 0)
        def _():
            across(g, start)

    def rest_of(g):
        @pl.when(jnp.logical_and(c > 0, even))
        def _():
            window_copy(g, 1, 0, c + 1).wait_recv()

        @pl.when(jnp.logical_not(even))
        def _():
            window_copy(g, 0, 0, c + 1).wait_recv()

    partners = [
        {"fc": (c + n // 2) % n},
        {"fc": c + 1 - 2 * (c % 2)},
        {"fr": (r + nr // 2) % nr},
        {"fr": r + 1 - 2 * (r % 2)},
    ]

    def columns(k):
        return pl.ds(pl.multiple_of(k * WIDTH, WIDTH), WIDTH)

    def level_copy(level, k):
        source = front_hbm if level == 0 else front
        return pltpu.make_async_remote_copy(
            src_ref=source.at[pl.ds(0, block), columns(k)],
            dst_ref=received.at[level, :, columns(k)],
            send_sem=level_send.at[level, k], recv_sem=level_recv.at[level, k],
            device_id=partners[level], device_id_type=MESH,
        )

    def panel_copy(k):
        part = pl.ds(pl.multiple_of(k * WIDTH, WIDTH), WIDTH)
        return pltpu.make_async_copy(panels_hbm.at[:, part], panels.at[:, part], panel_sem.at[k])

    def out_copy(k):
        return pltpu.make_async_copy(front.at[:, columns(k)], out_hbm.at[:, columns(k)], out_sem.at[k])

    def start_first_level(first, end):
        @pl.loop(first, end)
        def _(k):
            level_copy(0, k).start()

    @pl.when(c == 0)
    def _():
        for g in range(groups):
            chain(g)

    upper = c >= n // 2
    steps = pw // PIVOT
    hops = c // 2 + c % 2

    def relay_step(g):
        return 2 * (g + hops) - 1

    @pl.when(c >= 2)
    def _():
        start_first_level(0, EARLY)

    @pl.when(upper)
    def _():
        start_first_level(EARLY, chunks)

    front_load.start()

    @pl.loop(0, chunks)
    def _(k):
        panel_copy(k).start()

    for level in range(levels):
        wanted = maps_ref[pl.ds(level, 1), :]
        index = lax.broadcasted_iota(jnp.int32, (block, block), 0)
        move = jnp.where(index == wanted, 1.0, 0.0).T.astype(BF16)
        moves[level] = jnp.concatenate([move, move], axis=1)

    diag_load.wait()
    for copy in diag_copies:
        copy.wait()
    transposed = gathered[...]
    symmetric = 0.5 * (transposed + transposed.T)
    sub = lax.broadcasted_iota(jnp.int32, symmetric.shape, 0)
    lane = lax.broadcasted_iota(jnp.int32, symmetric.shape, 1)
    diagonal = jnp.where(sub == lane, symmetric, 0.0)
    scale_row = lax.rsqrt(jnp.sum(diagonal, axis=0, keepdims=True))
    scale_column = lax.rsqrt(jnp.sum(diagonal, axis=1, keepdims=True))
    work[...] = symmetric * scale_row * scale_column
    shared[r, pl.ds(pw, 8), :] = jnp.broadcast_to(scale_row, (8, pw))

    @pl.loop(0, steps)
    def _(i):
        pivot_step(work)

        for g in range(groups):
            @pl.when(jnp.logical_and(c > 0, i == relay_step(g)))
            def _():
                chain(g)

    shared[r, pl.ds(0, pw), :] = work[...]
    def inv_copy(index, slot, target):
        return pltpu.make_async_remote_copy(
            src_ref=shared.at[slot], dst_ref=shared.at[slot],
            send_sem=inv_send.at[index], recv_sem=inv_recv.at[index],
            device_id=target, device_id_type=MESH,
        )

    far, near = partners[2], partners[3]
    far_copy = inv_copy(0, r, far)
    near_copy = inv_copy(1, r, near)
    pass_copy = inv_copy(2, far["fr"], near)
    far_copy.start()
    near_copy.start()
    for g in range(groups):
        @pl.when(jnp.logical_and(c > 0, relay_step(g) >= steps))
        def _():
            chain(g)

        @pl.when(c == 0)
        def _():
            forwards(g, wait_send)
            across(g, start)

    @pl.when(jnp.logical_not(upper))
    def _():
        @pl.when(c < 2)
        def _():
            start_first_level(0, EARLY)

        start_first_level(EARLY, chunks)

    far_copy.wait_recv()
    pass_copy.start()
    for g in range(groups):
        rest_of(g)
    far_copy.wait_send()
    near_copy.wait()
    pass_copy.wait()

    def scaled(x, level):
        return x * shared[level, pl.ds(pw, 1), :]

    for level in range(levels):
        x_high, x_low = split(scaled(window[level], level))
        high, low = split(shared[level, pl.ds(0, pw), :])
        s = jnp.dot(
            jnp.concatenate([x_high, x_low, x_high], axis=1),
            jnp.concatenate([high, high, low], axis=0),
            preferred_element_type=F32,
        )
        high, low = split(s)
        factors[level] = jnp.concatenate([high, low, high], axis=1)
    front_load.wait()

    def update(level, k):
        high, low = split(scaled(panels[level, columns(k), :], level))
        return dot_t(factors[level], jnp.concatenate([high, high, low], axis=1))

    def stage(level, k):
        if level == 0:
            panel_copy(k).wait()
        total = update(level, k)
        top, below = pl.ds(0, block), pl.ds(block, rows - block)
        level_copy(level, k).wait()
        pair = jnp.concatenate(split(received[level, :, columns(k)]), axis=0)
        moved = jnp.dot(moves[level], pair, preferred_element_type=F32)
        front[top, columns(k)] = front[top, columns(k)] + moved - total[:block]
        if level + 1 < levels:
            level_copy(level + 1, k).start()
        front[below, columns(k)] = front[below, columns(k)] - total[block:]
        if level + 1 == levels:
            out_copy(k).start()

    @pl.loop(0, chunks + SKEW * (levels - 1))
    def _(t):
        for level in reversed(range(levels)):
            @pl.when(jnp.logical_and(t >= SKEW * level, t < chunks + SKEW * level))
            def _():
                stage(level, t - SKEW * level)

    for g in range(groups):
        @pl.when(c > 0)
        def _():
            forwards(g, wait_send)

        across(g, wait_send)

    @pl.loop(0, chunks)
    def _(k):
        out_copy(k).wait()


def body(front_slab, panels, diagonal_blocks, extend_maps):
    rows, cols = front_slab.shape
    levels, _, pw = panels.shape
    block = extend_maps.shape[3]
    n, nr = lax.axis_size("fc"), lax.axis_size("fr")
    chunks, groups = cols // WIDTH, rows // block
    mine = lax.dynamic_index_in_dim(diagonal_blocks, lax.axis_index("fr"), 0, keepdims=False).T
    anywhere = pl.BlockSpec(memory_space=pl.ANY)
    dma = pltpu.SemaphoreType.DMA
    return pl.pallas_call(
        functools.partial(kernel, n, nr),
        out_shape=jax.ShapeDtypeStruct((rows, cols), F32),
        in_specs=[anywhere, anywhere, anywhere, pl.BlockSpec(memory_space=pltpu.VMEM)],
        out_specs=anywhere,
        scratch_shapes=[
            pltpu.VMEM((rows, cols), F32),
            pltpu.VMEM(panels.shape, F32),
            pltpu.VMEM((pw, pw), F32),
            pltpu.VMEM((pw, pw), F32),
            pltpu.VMEM((levels, pw + 8, pw), F32),
            pltpu.VMEM((levels, rows, pw), F32),
            pltpu.VMEM((levels, rows, 3 * pw), BF16),
            pltpu.VMEM((levels, block, 2 * block), BF16),
            pltpu.VMEM((levels, block, cols), F32),
            dma((n - 1,)),
            dma((n - 1,)),
            dma((groups, 2, 2)),
            dma((groups, 2)),
            dma((groups,)),
            dma((nr - 1,)),
            dma((nr - 1,)),
            dma((levels, chunks)),
            dma((levels, chunks)),
            dma((2,)),
            dma((chunks,)),
            dma((chunks,)),
        ],
        compiler_params=pltpu.CompilerParams(
            collective_id=0, has_side_effects=True, vmem_limit_bytes=50 * 2**20
        ),
        cost_estimate=pl.CostEstimate(
            flops=6 * rows * cols * levels * pw, bytes_accessed=8 * rows * cols + 4 * panels.size, transcendentals=0
        ),
    )(front_slab, panels, mine, extend_maps.reshape(levels, block))


def solution(mesh):
    in_specs = (P("fr", "fc"), P(None, "fc", None), P(None, None, "fc"), P(None, "fr", "fc", None))
    return jax.shard_map(body, mesh=mesh, in_specs=in_specs, out_specs=P("fr", "fc"), check_vma=False)
```

```python
import functools

import jax
import jax.numpy as jnp
from jax import lax
from jax.experimental import pallas as pl
from jax.experimental.pallas import tpu as pltpu
from jax.sharding import PartitionSpec as P

HIGHEST = lax.Precision.HIGHEST
MESH = pl.DeviceIdType.MESH
F32, BF16 = jnp.float32, jnp.bfloat16
PIVOT = 32
WIDTH = 256
SKEW = 2


def split(x):
    high = x.astype(BF16)
    return high, (x - high.astype(F32)).astype(BF16)


def dot_t(a, b):
    return lax.dot_general(a, b, (((1,), (1,)), ((), ())), preferred_element_type=F32)


def exact_dot(a, b):
    return jnp.dot(a, b, precision=HIGHEST, preferred_element_type=F32)


def small_inverse(m):
    size, group = m.shape[0], 8
    shape = (group, size)
    sub = lax.broadcasted_iota(jnp.int32, shape, 0)
    lane = lax.broadcasted_iota(jnp.int32, shape, 1)
    parts = [m[i : i + group] for i in range(0, size, group)]

    def row_of(x, k):
        return jnp.broadcast_to(x[k : k + 1], shape)

    for q in range(size // group):
        spread = [
            [jnp.broadcast_to(part[:, q * group + j : q * group + j + 1], shape) for j in range(group)]
            for part in parts
        ]
        rows, columns = parts[q], list(spread[q])
        for k in range(group):
            at = q * group + k
            column = columns[k]
            scale = 1.0 / row_of(column, k)
            pivot_row = jnp.where(lane == at, scale, row_of(rows, k) * scale)
            rows = jnp.where(sub == k, pivot_row, jnp.where(lane == at, 0.0, rows) - column * pivot_row)
            for j in range(k + 1, group):
                other = row_of(columns[j], k) * scale
                columns[j] = jnp.where(sub == k, other, columns[j] - column * other)
        inside = jnp.logical_and(lane >= q * group, lane < (q + 1) * group)
        for i in range(len(parts)):
            if i != q:
                part = jnp.where(inside, 0.0, parts[i])
                for j in range(group):
                    part = part - spread[i][j] * row_of(rows, j)
                parts[i] = part
        parts[q] = rows
    return jnp.concatenate(parts, axis=0)


def pivot_step(work):
    size = work.shape[0]
    w = work[...]
    inverse = small_inverse(w[:PIVOT, :PIVOT])
    lane = lax.broadcasted_iota(jnp.int32, (PIVOT, size), 1)
    sub = lax.broadcasted_iota(jnp.int32, (PIVOT, size), 0)
    top = jnp.where(lane < PIVOT, jnp.where(lane == sub, 1.0, 0.0), w[:PIVOT])
    top = exact_dot(inverse, top)
    below = w[PIVOT:]
    lane = lax.broadcasted_iota(jnp.int32, below.shape, 1)
    below = jnp.where(lane < PIVOT, 0.0, below) - exact_dot(below[:, :PIVOT], top)
    turn = lambda x: jnp.concatenate([x[:, PIVOT:], x[:, :PIVOT]], axis=1)
    work[pl.ds(0, size - PIVOT), :] = turn(below)
    work[pl.ds(size - PIVOT, PIVOT), :] = turn(top)


def kernel(
    n, nr, front_hbm, panels_hbm, diag_hbm, maps_ref, out_hbm,
    front, panels, gathered, work, shared, window, factors, moves, received,
    diag_send, diag_recv, window_send, window_recv, window_load, inv_send, inv_recv,
    level_send, level_recv, load_sem, front_sem, panel_sem, out_sem,
):
    c, r = lax.axis_index("fc"), lax.axis_index("fr")
    levels, pw = panels.shape[0], panels.shape[2]
    chunks, rows, _ = front.shape
    cols = chunks * WIDTH
    block = received.shape[2]
    groups = rows // block
    share = pw // n
    half = levels // 2
    even = c % 2 == 0

    barrier = pltpu.get_barrier_semaphore()
    for d in range(1, n):
        pl.semaphore_signal(barrier, inc=1, device_id={"fc": (c + d) % n}, device_id_type=MESH)
    for d in range(1, nr):
        pl.semaphore_signal(barrier, inc=1, device_id={"fr": (r + d) % nr}, device_id_type=MESH)
    own_window = []
    for g in range(groups):
        start = pl.multiple_of((r * rows) % cols + g * block, block)
        own_window.append(pltpu.make_async_copy(
            panels_hbm.at[:, pl.ds(start, block)], window.at[:, pl.ds(g * block, block)], window_load.at[g]
        ))
    diag_rows = pl.ds(pl.multiple_of(c * share, 8), share)
    diag_load = pltpu.make_async_copy(diag_hbm, gathered.at[diag_rows], load_sem)
    diag_load.start()

    @pl.when(c == 0)
    def _():
        for copy in own_window:
            copy.start()

    def columns(k):
        return pl.ds(pl.multiple_of(k * WIDTH, WIDTH), WIDTH)

    def front_copy(k):
        return pltpu.make_async_copy(front_hbm.at[:, columns(k)], front.at[k], front_sem.at[k])

    @pl.loop(0, chunks)
    def _(k):
        front_copy(k).start()

    pl.semaphore_wait(barrier, n - 1 + nr - 1)

    diag_copies = []
    for d in range(1, n):
        diag_copies.append(pltpu.make_async_remote_copy(
            src_ref=diag_hbm, dst_ref=gathered.at[diag_rows],
            send_sem=diag_send.at[d - 1], recv_sem=diag_recv.at[d - 1],
            device_id={"fc": (c + d) % n}, device_id_type=MESH,
        ))
    for copy in diag_copies:
        copy.start()

    def window_copy(g, h, way, target):
        part = window.at[pl.ds(h * half, half), pl.ds(g * block, block)]
        return pltpu.make_async_remote_copy(
            src_ref=part, dst_ref=part,
            send_sem=window_send.at[g, h, way], recv_sem=window_recv.at[g, h],
            device_id={"fc": target % n}, device_id_type=MESH,
        )

    def across(g, act):
        @pl.when(even)
        def _():
            act(window_copy(g, 0, 1, c + 1))

    def forwards(g, act):
        @pl.when(even)
        def _():
            @pl.when(c + 2 < n)
            def _():
                act(window_copy(g, 0, 0, c + 2))

        @pl.when(c == 0)
        def _():
            act(window_copy(g, 1, 0, 1 + c))

        @pl.when(jnp.logical_not(even))
        def _():
            @pl.when(c + 2 < n)
            def _():
                act(window_copy(g, 1, 0, c + 2))

            @pl.when(c >= 3)
            def _():
                act(window_copy(g, 1, 1, c - 1))

    def start(copy):
        copy.start()

    def wait_send(copy):
        copy.wait_send()

    def chain(g):
        @pl.when(c == 0)
        def _():
            own_window[g].wait()

        @pl.when(jnp.logical_and(c > 0, even))
        def _():
            window_copy(g, 0, 0, c + 1).wait_recv()

        @pl.when(jnp.logical_not(even))
        def _():
            window_copy(g, 1, 0, c + 1).wait_recv()

        forwards(g, start)

        @pl.when(c > 0)
        def _():
            across(g, start)

    def rest_of(g):
        @pl.when(jnp.logical_and(c > 0, even))
        def _():
            window_copy(g, 1, 0, c + 1).wait_recv()

        @pl.when(jnp.logical_not(even))
        def _():
            window_copy(g, 0, 0, c + 1).wait_recv()

    partners = [
        {"fc": (c + n // 2) % n},
        {"fc": c + 1 - 2 * (c % 2)},
        {"fr": (r + nr // 2) % nr},
        {"fr": r + 1 - 2 * (r % 2)},
    ]

    def level_copy(level, k):
        return pltpu.make_async_remote_copy(
            src_ref=front.at[k, pl.ds(0, block)],
            dst_ref=received.at[level, k],
            send_sem=level_send.at[level, k], recv_sem=level_recv.at[level, k],
            device_id=partners[level], device_id_type=MESH,
        )

    def panel_copy(k):
        part = pl.ds(pl.multiple_of(k * WIDTH, WIDTH), WIDTH)
        return pltpu.make_async_copy(panels_hbm.at[:, part], panels.at[:, part], panel_sem.at[k])

    def out_copy(k):
        return pltpu.make_async_copy(front.at[k], out_hbm.at[:, columns(k)], out_sem.at[k])

    def start_first_level(first, end):
        @pl.loop(first, end)
        def _(k):
            level_copy(0, k).start()

    @pl.when(c == 0)
    def _():
        for g in range(groups):
            chain(g)

    @pl.loop(0, chunks)
    def _(k):
        front_copy(k).wait()

    upper = c >= n // 2
    steps = pw // PIVOT
    hops = c // 2 + c % 2

    def relay_step(g):
        return g + hops

    lower_relay = jnp.logical_and(c > 0, jnp.logical_not(upper))

    @pl.when(upper)
    def _():
        start_first_level(0, chunks)

    @pl.loop(0, chunks)
    def _(k):
        panel_copy(k).start()

    for level in range(levels):
        wanted = maps_ref[pl.ds(level, 1), :]
        index = lax.broadcasted_iota(jnp.int32, (block, block), 0)
        move = jnp.where(index == wanted, 1.0, 0.0).T.astype(BF16)
        moves[level] = jnp.concatenate([move, move], axis=1)

    diag_load.wait()
    for copy in diag_copies:
        copy.wait()
    transposed = gathered[...]
    symmetric = 0.5 * (transposed + transposed.T)
    sub = lax.broadcasted_iota(jnp.int32, symmetric.shape, 0)
    lane = lax.broadcasted_iota(jnp.int32, symmetric.shape, 1)
    diagonal = jnp.where(sub == lane, symmetric, 0.0)
    scale_row = lax.rsqrt(jnp.sum(diagonal, axis=0, keepdims=True))
    scale_column = lax.rsqrt(jnp.sum(diagonal, axis=1, keepdims=True))
    work[...] = symmetric * scale_row * scale_column
    shared[r, pl.ds(pw, 8), :] = jnp.broadcast_to(scale_row, (8, pw))

    @pl.loop(0, steps)
    def _(i):
        pivot_step(work)

        for g in range(groups):
            @pl.when(jnp.logical_and(c > 0, i == relay_step(g)))
            def _():
                chain(g)

            @pl.when(jnp.logical_and(c == 0, i == steps - groups + g))
            def _():
                across(g, start)

        @pl.when(jnp.logical_and(lower_relay, i == relay_step(groups - 1)))
        def _():
            start_first_level(0, chunks)

    shared[r, pl.ds(0, pw), :] = work[...]
    def inv_copy(index, slot, target):
        return pltpu.make_async_remote_copy(
            src_ref=shared.at[slot], dst_ref=shared.at[slot],
            send_sem=inv_send.at[index], recv_sem=inv_recv.at[index],
            device_id=target, device_id_type=MESH,
        )

    far, near = partners[2], partners[3]
    far_copy = inv_copy(0, r, far)
    near_copy = inv_copy(1, r, near)
    pass_copy = inv_copy(2, far["fr"], near)
    far_copy.start()
    near_copy.start()
    for g in range(groups):
        @pl.when(jnp.logical_and(c > 0, relay_step(g) >= steps))
        def _():
            chain(g)

        @pl.when(c == 0)
        def _():
            forwards(g, wait_send)

    @pl.when(jnp.logical_or(c == 0, jnp.logical_and(lower_relay, relay_step(groups - 1) >= steps)))
    def _():
        start_first_level(0, chunks)

    far_copy.wait_recv()
    pass_copy.start()
    for g in range(groups):
        rest_of(g)
    far_copy.wait_send()
    near_copy.wait()
    pass_copy.wait()

    def scaled(x, level):
        return x * shared[level, pl.ds(pw, 1), :]

    for level in range(levels):
        x_high, x_low = split(scaled(window[level], level))
        high, low = split(shared[level, pl.ds(0, pw), :])
        s = jnp.dot(
            jnp.concatenate([x_high, x_low, x_high], axis=1),
            jnp.concatenate([high, high, low], axis=0),
            preferred_element_type=F32,
        )
        high, low = split(s)
        factors[level] = jnp.concatenate([high, low, high], axis=1)
    def update(level, k):
        high, low = split(scaled(panels[level, columns(k), :], level))
        return dot_t(factors[level], jnp.concatenate([high, high, low], axis=1))

    def stage(level, k):
        if level == 0:
            panel_copy(k).wait()
        total = update(level, k)
        top, below = pl.ds(0, block), pl.ds(block, rows - block)
        level_copy(level, k).wait()
        pair = jnp.concatenate(split(received[level, k]), axis=0)
        moved = jnp.dot(moves[level], pair, preferred_element_type=F32)
        front[k, top, :] = front[k, top, :] + moved - total[:block]
        if level + 1 < levels:
            level_copy(level + 1, k).start()
        front[k, below, :] = front[k, below, :] - total[block:]
        if level + 1 == levels:
            out_copy(k).start()

    @pl.loop(0, chunks + SKEW * (levels - 1))
    def _(t):
        for level in reversed(range(levels)):
            @pl.when(jnp.logical_and(t >= SKEW * level, t < chunks + SKEW * level))
            def _():
                stage(level, t - SKEW * level)

    for g in range(groups):
        @pl.when(c > 0)
        def _():
            forwards(g, wait_send)

        across(g, wait_send)

    @pl.loop(0, chunks)
    def _(k):
        out_copy(k).wait()


def body(front_slab, panels, diagonal_blocks, extend_maps):
    rows, cols = front_slab.shape
    levels, _, pw = panels.shape
    block = extend_maps.shape[3]
    n, nr = lax.axis_size("fc"), lax.axis_size("fr")
    chunks, groups = cols // WIDTH, rows // block
    mine = lax.dynamic_index_in_dim(diagonal_blocks, lax.axis_index("fr"), 0, keepdims=False).T
    anywhere = pl.BlockSpec(memory_space=pl.ANY)
    dma = pltpu.SemaphoreType.DMA
    return pl.pallas_call(
        functools.partial(kernel, n, nr),
        out_shape=jax.ShapeDtypeStruct((rows, cols), F32),
        in_specs=[anywhere, anywhere, anywhere, pl.BlockSpec(memory_space=pltpu.VMEM)],
        out_specs=anywhere,
        scratch_shapes=[
            pltpu.VMEM((chunks, rows, WIDTH), F32),
            pltpu.VMEM(panels.shape, F32),
            pltpu.VMEM((pw, pw), F32),
            pltpu.VMEM((pw, pw), F32),
            pltpu.VMEM((levels, pw + 8, pw), F32),
            pltpu.VMEM((levels, rows, pw), F32),
            pltpu.VMEM((levels, rows, 3 * pw), BF16),
            pltpu.VMEM((levels, block, 2 * block), BF16),
            pltpu.VMEM((levels, chunks, block, WIDTH), F32),
            dma((n - 1,)),
            dma((n - 1,)),
            dma((groups, 2, 2)),
            dma((groups, 2)),
            dma((groups,)),
            dma((nr - 1,)),
            dma((nr - 1,)),
            dma((levels, chunks)),
            dma((levels, chunks)),
            dma,
            dma((chunks,)),
            dma((chunks,)),
            dma((chunks,)),
        ],
        compiler_params=pltpu.CompilerParams(
            collective_id=0, has_side_effects=True, vmem_limit_bytes=50 * 2**20
        ),
        cost_estimate=pl.CostEstimate(
            flops=6 * rows * cols * levels * pw, bytes_accessed=8 * rows * cols + 4 * panels.size, transcendentals=0
        ),
    )(front_slab, panels, mine, extend_maps.reshape(levels, block))


def solution(mesh):
    in_specs = (P("fr", "fc"), P(None, "fc", None), P(None, None, "fc"), P(None, "fr", "fc", None))
    return jax.shard_map(body, mesh=mesh, in_specs=in_specs, out_specs=P("fr", "fc"), check_vma=False)
```

```python
import functools

import jax
import jax.numpy as jnp
from jax import lax
from jax.experimental import pallas as pl
from jax.experimental.pallas import tpu as pltpu
from jax.sharding import PartitionSpec as P

HIGHEST = lax.Precision.HIGHEST
MESH = pl.DeviceIdType.MESH
F32, BF16 = jnp.float32, jnp.bfloat16
PIVOT = 32
WIDTH = 256
SKEW = 2
OPEN = 4


def split(x):
    high = x.astype(BF16)
    return high, (x - high.astype(F32)).astype(BF16)


def dot_t(a, b):
    return lax.dot_general(a, b, (((1,), (1,)), ((), ())), preferred_element_type=F32)


def exact_dot(a, b):
    return jnp.dot(a, b, precision=HIGHEST, preferred_element_type=F32)


def small_inverse(m):
    size, group = m.shape[0], 8
    shape = (group, size)
    sub = lax.broadcasted_iota(jnp.int32, shape, 0)
    lane = lax.broadcasted_iota(jnp.int32, shape, 1)
    parts = [m[i : i + group] for i in range(0, size, group)]

    def row_of(x, k):
        return jnp.broadcast_to(x[k : k + 1], shape)

    for q in range(size // group):
        spread = [
            [jnp.broadcast_to(part[:, q * group + j : q * group + j + 1], shape) for j in range(group)]
            for part in parts
        ]
        rows, columns = parts[q], list(spread[q])
        for k in range(group):
            at = q * group + k
            column = columns[k]
            scale = 1.0 / row_of(column, k)
            pivot_row = jnp.where(lane == at, scale, row_of(rows, k) * scale)
            rows = jnp.where(sub == k, pivot_row, jnp.where(lane == at, 0.0, rows) - column * pivot_row)
            for j in range(k + 1, group):
                other = row_of(columns[j], k) * scale
                columns[j] = jnp.where(sub == k, other, columns[j] - column * other)
        inside = jnp.logical_and(lane >= q * group, lane < (q + 1) * group)
        for i in range(len(parts)):
            if i != q:
                part = jnp.where(inside, 0.0, parts[i])
                for j in range(group):
                    part = part - spread[i][j] * row_of(rows, j)
                parts[i] = part
        parts[q] = rows
    return jnp.concatenate(parts, axis=0)


def pivot_step(work):
    size = work.shape[0]
    w = work[...]
    inverse = small_inverse(w[:PIVOT, :PIVOT])
    lane = lax.broadcasted_iota(jnp.int32, (PIVOT, size), 1)
    sub = lax.broadcasted_iota(jnp.int32, (PIVOT, size), 0)
    top = jnp.where(lane < PIVOT, jnp.where(lane == sub, 1.0, 0.0), w[:PIVOT])
    top = exact_dot(inverse, top)
    below = w[PIVOT:]
    lane = lax.broadcasted_iota(jnp.int32, below.shape, 1)
    below = jnp.where(lane < PIVOT, 0.0, below) - exact_dot(below[:, :PIVOT], top)
    turn = lambda x: jnp.concatenate([x[:, PIVOT:], x[:, :PIVOT]], axis=1)
    work[pl.ds(0, size - PIVOT), :] = turn(below)
    work[pl.ds(size - PIVOT, PIVOT), :] = turn(top)


def kernel(
    n, nr, front_hbm, panels_hbm, diag_hbm, maps_ref, out_hbm,
    front, panels, gathered, work, shared, window, factors, moves, received,
    diag_send, diag_recv, window_send, window_recv, window_load, inv_send, inv_recv,
    level_send, level_recv, load_sem, front_sem, panel_sem, out_sem,
):
    c, r = lax.axis_index("fc"), lax.axis_index("fr")
    levels, pw = panels.shape[0], panels.shape[2]
    chunks, rows, _ = front.shape
    cols = chunks * WIDTH
    block = received.shape[2]
    groups = rows // block
    share = pw // n
    half = levels // 2
    even = c % 2 == 0

    barrier = pltpu.get_barrier_semaphore()
    for d in range(1, n):
        pl.semaphore_signal(barrier, inc=1, device_id={"fc": (c + d) % n}, device_id_type=MESH)
    for d in range(1, nr):
        pl.semaphore_signal(barrier, inc=1, device_id={"fr": (r + d) % nr}, device_id_type=MESH)
    own_window = []
    for g in range(groups):
        start = pl.multiple_of((r * rows) % cols + g * block, block)
        own_window.append(pltpu.make_async_copy(
            panels_hbm.at[:, pl.ds(start, block)], window.at[:, pl.ds(g * block, block)], window_load.at[g]
        ))
    diag_rows = pl.ds(pl.multiple_of(c * share, 8), share)
    diag_load = pltpu.make_async_copy(diag_hbm, gathered.at[diag_rows], load_sem)
    diag_load.start()

    @pl.when(c == 0)
    def _():
        for copy in own_window:
            copy.start()

    def columns(k):
        return pl.ds(pl.multiple_of(k * WIDTH, WIDTH), WIDTH)

    def front_copy(k):
        return pltpu.make_async_copy(front_hbm.at[:, columns(k)], front.at[k], front_sem.at[k])

    @pl.loop(0, chunks)
    def _(k):
        front_copy(k).start()

    pl.semaphore_wait(barrier, n - 1 + nr - 1)

    diag_copies = []
    for d in range(1, n):
        diag_copies.append(pltpu.make_async_remote_copy(
            src_ref=diag_hbm, dst_ref=gathered.at[diag_rows],
            send_sem=diag_send.at[d - 1], recv_sem=diag_recv.at[d - 1],
            device_id={"fc": (c + d) % n}, device_id_type=MESH,
        ))
    for copy in diag_copies:
        copy.start()

    def window_copy(g, h, way, target):
        part = window.at[pl.ds(h * half, half), pl.ds(g * block, block)]
        return pltpu.make_async_remote_copy(
            src_ref=part, dst_ref=part,
            send_sem=window_send.at[g, h, way], recv_sem=window_recv.at[g, h],
            device_id={"fc": target % n}, device_id_type=MESH,
        )

    def across(g, act):
        @pl.when(even)
        def _():
            act(window_copy(g, 0, 1, c + 1))

    def forwards(g, act):
        @pl.when(even)
        def _():
            @pl.when(c + 2 < n)
            def _():
                act(window_copy(g, 0, 0, c + 2))

        @pl.when(c == 0)
        def _():
            act(window_copy(g, 1, 0, 1 + c))

        @pl.when(jnp.logical_not(even))
        def _():
            @pl.when(c + 2 < n)
            def _():
                act(window_copy(g, 1, 0, c + 2))

            @pl.when(c >= 3)
            def _():
                act(window_copy(g, 1, 1, c - 1))

    def start(copy):
        copy.start()

    def wait_send(copy):
        copy.wait_send()

    def chain(g):
        @pl.when(c == 0)
        def _():
            own_window[g].wait()

        @pl.when(jnp.logical_and(c > 0, even))
        def _():
            window_copy(g, 0, 0, c + 1).wait_recv()

        @pl.when(jnp.logical_not(even))
        def _():
            window_copy(g, 1, 0, c + 1).wait_recv()

        forwards(g, start)

        @pl.when(c > 0)
        def _():
            across(g, start)

    def rest_of(g):
        @pl.when(jnp.logical_and(c > 0, even))
        def _():
            window_copy(g, 1, 0, c + 1).wait_recv()

        @pl.when(jnp.logical_not(even))
        def _():
            window_copy(g, 0, 0, c + 1).wait_recv()

    partners = [
        {"fc": (c + n // 2) % n},
        {"fc": c + 1 - 2 * (c % 2)},
        {"fr": (r + nr // 2) % nr},
        {"fr": r + 1 - 2 * (r % 2)},
    ]

    def level_copy(level, k):
        return pltpu.make_async_remote_copy(
            src_ref=front.at[k, pl.ds(0, block)],
            dst_ref=received.at[level, k],
            send_sem=level_send.at[level, k], recv_sem=level_recv.at[level, k],
            device_id=partners[level], device_id_type=MESH,
        )

    def panel_copy(k):
        part = pl.ds(pl.multiple_of(k * WIDTH, WIDTH), WIDTH)
        return pltpu.make_async_copy(panels_hbm.at[:, part], panels.at[:, part], panel_sem.at[k])

    def out_copy(k):
        return pltpu.make_async_copy(front.at[k], out_hbm.at[:, columns(k)], out_sem.at[k])

    def start_first_level(first, end):
        @pl.loop(first, end)
        def _(k):
            level_copy(0, k).start()

    @pl.when(c == 0)
    def _():
        chain(0)

    @pl.loop(0, chunks)
    def _(k):
        front_copy(k).wait()

    upper = c >= n // 2
    steps = pw // PIVOT
    hops = c // 2 + c % 2

    def relay_step(g):
        return g + hops

    @pl.when(upper)
    def _():
        start_first_level(0, OPEN)

    @pl.loop(0, chunks)
    def _(k):
        panel_copy(k).start()

    for level in range(levels):
        wanted = maps_ref[pl.ds(level, 1), :]
        index = lax.broadcasted_iota(jnp.int32, (block, block), 0)
        move = jnp.where(index == wanted, 1.0, 0.0).T.astype(BF16)
        moves[level] = jnp.concatenate([move, move], axis=1)

    diag_load.wait()
    for copy in diag_copies:
        copy.wait()
    transposed = gathered[...]
    symmetric = 0.5 * (transposed + transposed.T)
    sub = lax.broadcasted_iota(jnp.int32, symmetric.shape, 0)
    lane = lax.broadcasted_iota(jnp.int32, symmetric.shape, 1)
    diagonal = jnp.where(sub == lane, symmetric, 0.0)
    scale_row = lax.rsqrt(jnp.sum(diagonal, axis=0, keepdims=True))
    scale_column = lax.rsqrt(jnp.sum(diagonal, axis=1, keepdims=True))
    work[...] = symmetric * scale_row * scale_column
    shared[r, pl.ds(pw, 8), :] = jnp.broadcast_to(scale_row, (8, pw))

    @pl.loop(0, steps)
    def _(i):
        pivot_step(work)

        for g in range(groups):
            @pl.when(jnp.logical_and(c > 0, i == relay_step(g)))
            def _():
                chain(g)

            @pl.when(jnp.logical_and(c == 0, i == steps - groups + g))
            def _():
                across(g, start)

            if g:
                @pl.when(jnp.logical_and(c == 0, i == g - 1))
                def _():
                    forwards(g - 1, wait_send)
                    chain(g)

        @pl.when(jnp.logical_and(upper, i % 2 == 1))
        def _():
            level_copy(0, i // 2).wait_send()
            level_copy(0, i // 2 + OPEN).start()

        @pl.when(jnp.logical_and(jnp.logical_not(upper), i == steps // 2))
        def _():
            start_first_level(0, OPEN)

        @pl.when(jnp.logical_and(jnp.logical_not(upper), i == steps - 1))
        def _():
            start_first_level(OPEN, 2 * OPEN)

    shared[r, pl.ds(0, pw), :] = work[...]
    def inv_copy(index, slot, target):
        return pltpu.make_async_remote_copy(
            src_ref=shared.at[slot], dst_ref=shared.at[slot],
            send_sem=inv_send.at[index], recv_sem=inv_recv.at[index],
            device_id=target, device_id_type=MESH,
        )

    far, near = partners[2], partners[3]
    far_copy = inv_copy(0, r, far)
    near_copy = inv_copy(1, r, near)
    pass_copy = inv_copy(2, far["fr"], near)
    far_copy.start()
    near_copy.start()
    for g in range(groups):
        @pl.when(jnp.logical_and(c > 0, relay_step(g) >= steps))
        def _():
            chain(g)

    @pl.when(c == 0)
    def _():
        forwards(groups - 1, wait_send)

    far_copy.wait_recv()
    pass_copy.start()
    for g in range(groups):
        rest_of(g)
    far_copy.wait_send()
    near_copy.wait()
    pass_copy.wait()

    def scaled(x, level):
        return x * shared[level, pl.ds(pw, 1), :]

    for level in range(levels):
        x_high, x_low = split(scaled(window[level], level))
        high, low = split(shared[level, pl.ds(0, pw), :])
        s = jnp.dot(
            jnp.concatenate([x_high, x_low, x_high], axis=1),
            jnp.concatenate([high, high, low], axis=0),
            preferred_element_type=F32,
        )
        high, low = split(s)
        factors[level] = jnp.concatenate([high, low, high], axis=1)
    def update(level, k):
        high, low = split(scaled(panels[level, columns(k), :], level))
        return dot_t(factors[level], jnp.concatenate([high, high, low], axis=1))

    @pl.when(jnp.logical_not(upper))
    def _():
        @pl.loop(0, OPEN)
        def _(k):
            level_copy(0, k).wait_send()

    def arrive(level, k):
        if level == 0:
            panel_copy(k).wait()
            level_copy(level, k).wait_recv()

            @pl.when(k >= 2 * OPEN)
            def _():
                level_copy(level, k).wait_send()

            @pl.when(k + 2 * OPEN < chunks)
            def _():
                level_copy(level, k + OPEN).wait_send()
                level_copy(level, k + 2 * OPEN).start()

            @pl.when(jnp.logical_and(k + 2 * OPEN >= chunks, k < OPEN))
            def _():
                level_copy(level, k + OPEN).wait_send()
        else:
            level_copy(level, k).wait()

    def stage(level, k):
        total = update(level, k)
        top, below = pl.ds(0, block), pl.ds(block, rows - block)
        pair = jnp.concatenate(split(received[level, k]), axis=0)
        moved = jnp.dot(moves[level], pair, preferred_element_type=F32)
        front[k, top, :] = front[k, top, :] + moved - total[:block]
        front[k, below, :] = front[k, below, :] - total[block:]

    def leave(level, k):
        if level + 1 < levels:
            level_copy(level + 1, k).start()
        else:
            out_copy(k).start()

    marks = sorted({SKEW * level + end for level in range(levels) for end in (0, chunks)})
    for first, end in zip(marks, marks[1:]):
        active = [x for x in reversed(range(levels)) if SKEW * x <= first < chunks + SKEW * x]

        @pl.loop(first, end)
        def _(t, active=active):
            for act in (arrive, stage, leave):
                for level in active:
                    act(level, t - SKEW * level)

    for g in range(groups):
        @pl.when(c > 0)
        def _():
            forwards(g, wait_send)

        across(g, wait_send)

    @pl.loop(0, chunks)
    def _(k):
        out_copy(k).wait()


def body(front_slab, panels, diagonal_blocks, extend_maps):
    rows, cols = front_slab.shape
    levels, _, pw = panels.shape
    block = extend_maps.shape[3]
    n, nr = lax.axis_size("fc"), lax.axis_size("fr")
    chunks, groups = cols // WIDTH, rows // block
    mine = lax.dynamic_index_in_dim(diagonal_blocks, lax.axis_index("fr"), 0, keepdims=False).T
    anywhere = pl.BlockSpec(memory_space=pl.ANY)
    dma = pltpu.SemaphoreType.DMA
    return pl.pallas_call(
        functools.partial(kernel, n, nr),
        out_shape=jax.ShapeDtypeStruct((rows, cols), F32),
        in_specs=[anywhere, anywhere, anywhere, pl.BlockSpec(memory_space=pltpu.VMEM)],
        out_specs=anywhere,
        scratch_shapes=[
            pltpu.VMEM((chunks, rows, WIDTH), F32),
            pltpu.VMEM(panels.shape, F32),
            pltpu.VMEM((pw, pw), F32),
            pltpu.VMEM((pw, pw), F32),
            pltpu.VMEM((levels, pw + 8, pw), F32),
            pltpu.VMEM((levels, rows, pw), F32),
            pltpu.VMEM((levels, rows, 3 * pw), BF16),
            pltpu.VMEM((levels, block, 2 * block), BF16),
            pltpu.VMEM((levels, chunks, block, WIDTH), F32),
            dma((n - 1,)),
            dma((n - 1,)),
            dma((groups, 2, 2)),
            dma((groups, 2)),
            dma((groups,)),
            dma((nr - 1,)),
            dma((nr - 1,)),
            dma((levels, chunks)),
            dma((levels, chunks)),
            dma,
            dma((chunks,)),
            dma((chunks,)),
            dma((chunks,)),
        ],
        compiler_params=pltpu.CompilerParams(
            collective_id=0, has_side_effects=True, vmem_limit_bytes=50 * 2**20
        ),
        cost_estimate=pl.CostEstimate(
            flops=6 * rows * cols * levels * pw, bytes_accessed=8 * rows * cols + 4 * panels.size, transcendentals=0
        ),
    )(front_slab, panels, mine, extend_maps.reshape(levels, block))


def solution(mesh):
    in_specs = (P("fr", "fc"), P(None, "fc", None), P(None, None, "fc"), P(None, "fr", "fc", None))
    return jax.shard_map(body, mesh=mesh, in_specs=in_specs, out_specs=P("fr", "fc"), check_vma=False)
```

```python
import functools

import jax
import jax.numpy as jnp
from jax import lax
from jax.experimental import pallas as pl
from jax.experimental.pallas import tpu as pltpu
from jax.sharding import PartitionSpec as P

HIGHEST = lax.Precision.HIGHEST
MESH = pl.DeviceIdType.MESH
F32, BF16 = jnp.float32, jnp.bfloat16
PIVOT = 32
WIDTH = 256
SKEW = 2
OPEN = 4
HOLD = 2


def split(x):
    high = x.astype(BF16)
    return high, (x - high.astype(F32)).astype(BF16)


def dot_t(a, b):
    return lax.dot_general(a, b, (((1,), (1,)), ((), ())), preferred_element_type=F32)


def exact_dot(a, b):
    return jnp.dot(a, b, precision=HIGHEST, preferred_element_type=F32)


def small_inverse(m):
    size, group = m.shape[0], 8
    shape = (group, size)
    sub = lax.broadcasted_iota(jnp.int32, shape, 0)
    lane = lax.broadcasted_iota(jnp.int32, shape, 1)
    parts = [m[i : i + group] for i in range(0, size, group)]

    def row_of(x, k):
        return jnp.broadcast_to(x[k : k + 1], shape)

    for q in range(size // group):
        spread = [
            [jnp.broadcast_to(part[:, q * group + j : q * group + j + 1], shape) for j in range(group)]
            for part in parts
        ]
        rows, columns = parts[q], list(spread[q])
        for k in range(group):
            at = q * group + k
            column = columns[k]
            scale = 1.0 / row_of(column, k)
            pivot_row = jnp.where(lane == at, scale, row_of(rows, k) * scale)
            rows = jnp.where(sub == k, pivot_row, jnp.where(lane == at, 0.0, rows) - column * pivot_row)
            for j in range(k + 1, group):
                other = row_of(columns[j], k) * scale
                columns[j] = jnp.where(sub == k, other, columns[j] - column * other)
        inside = jnp.logical_and(lane >= q * group, lane < (q + 1) * group)
        for i in range(len(parts)):
            if i != q:
                part = jnp.where(inside, 0.0, parts[i])
                for j in range(group):
                    part = part - spread[i][j] * row_of(rows, j)
                parts[i] = part
        parts[q] = rows
    return jnp.concatenate(parts, axis=0)


def pivot_step(work):
    size = work.shape[0]
    w = work[...]
    inverse = small_inverse(w[:PIVOT, :PIVOT])
    lane = lax.broadcasted_iota(jnp.int32, (PIVOT, size), 1)
    sub = lax.broadcasted_iota(jnp.int32, (PIVOT, size), 0)
    top = jnp.where(lane < PIVOT, jnp.where(lane == sub, 1.0, 0.0), w[:PIVOT])
    top = exact_dot(inverse, top)
    below = w[PIVOT:]
    lane = lax.broadcasted_iota(jnp.int32, below.shape, 1)
    below = jnp.where(lane < PIVOT, 0.0, below) - exact_dot(below[:, :PIVOT], top)
    turn = lambda x: jnp.concatenate([x[:, PIVOT:], x[:, :PIVOT]], axis=1)
    work[pl.ds(0, size - PIVOT), :] = turn(below)
    work[pl.ds(size - PIVOT, PIVOT), :] = turn(top)


def kernel(
    n, nr, front_hbm, panels_hbm, diag_hbm, maps_ref, out_hbm,
    front, panels, gathered, work, shared, window, factors, moves, received,
    diag_send, diag_recv, window_send, window_recv, window_load, inv_send, inv_recv,
    level_send, level_recv, load_sem, front_sem, panel_sem, out_sem,
):
    c, r = lax.axis_index("fc"), lax.axis_index("fr")
    levels, pw = panels.shape[0], panels.shape[2]
    chunks, rows, _ = front.shape
    cols = chunks * WIDTH
    block = received.shape[2]
    groups = rows // block
    share = pw // n
    half = levels // 2
    even = c % 2 == 0

    barrier = pltpu.get_barrier_semaphore()
    for d in range(1, n):
        pl.semaphore_signal(barrier, inc=1, device_id={"fc": (c + d) % n}, device_id_type=MESH)
    for d in range(1, nr):
        pl.semaphore_signal(barrier, inc=1, device_id={"fr": (r + d) % nr}, device_id_type=MESH)
    own_window = []
    for g in range(groups):
        start = pl.multiple_of((r * rows) % cols + g * block, block)
        own_window.append(pltpu.make_async_copy(
            panels_hbm.at[:, pl.ds(start, block)], window.at[:, pl.ds(g * block, block)], window_load.at[g]
        ))
    diag_rows = pl.ds(pl.multiple_of(c * share, 8), share)
    diag_load = pltpu.make_async_copy(diag_hbm, gathered.at[diag_rows], load_sem)
    diag_load.start()

    @pl.when(c == 0)
    def _():
        for copy in own_window:
            copy.start()

    def columns(k):
        return pl.ds(pl.multiple_of(k * WIDTH, WIDTH), WIDTH)

    def front_copy(k):
        return pltpu.make_async_copy(front_hbm.at[:, columns(k)], front.at[k], front_sem.at[k])

    @pl.loop(0, chunks)
    def _(k):
        front_copy(k).start()

    pl.semaphore_wait(barrier, n - 1 + nr - 1)

    diag_copies = []
    for d in range(1, n):
        diag_copies.append(pltpu.make_async_remote_copy(
            src_ref=diag_hbm, dst_ref=gathered.at[diag_rows],
            send_sem=diag_send.at[d - 1], recv_sem=diag_recv.at[d - 1],
            device_id={"fc": (c + d) % n}, device_id_type=MESH,
        ))
    for copy in diag_copies:
        copy.start()

    def window_copy(g, h, way, target):
        part = window.at[pl.ds(h * half, half), pl.ds(g * block, block)]
        return pltpu.make_async_remote_copy(
            src_ref=part, dst_ref=part,
            send_sem=window_send.at[g, h, way], recv_sem=window_recv.at[g, h],
            device_id={"fc": target % n}, device_id_type=MESH,
        )

    def across(g, act):
        @pl.when(even)
        def _():
            act(window_copy(g, 0, 1, c + 1))

    def forwards(g, act):
        @pl.when(even)
        def _():
            @pl.when(c + 2 < n)
            def _():
                act(window_copy(g, 0, 0, c + 2))

        @pl.when(c == 0)
        def _():
            act(window_copy(g, 1, 0, 1 + c))

        @pl.when(jnp.logical_not(even))
        def _():
            @pl.when(c + 2 < n)
            def _():
                act(window_copy(g, 1, 0, c + 2))

            @pl.when(c >= 3)
            def _():
                act(window_copy(g, 1, 1, c - 1))

    def start(copy):
        copy.start()

    def wait_send(copy):
        copy.wait_send()

    def chain(g):
        @pl.when(c == 0)
        def _():
            own_window[g].wait()

        @pl.when(jnp.logical_and(c > 0, even))
        def _():
            window_copy(g, 0, 0, c + 1).wait_recv()

        @pl.when(jnp.logical_not(even))
        def _():
            window_copy(g, 1, 0, c + 1).wait_recv()

        forwards(g, start)

        @pl.when(c > 0)
        def _():
            across(g, start)

    def rest_of(g):
        @pl.when(jnp.logical_and(c > 0, even))
        def _():
            window_copy(g, 1, 0, c + 1).wait_recv()

        @pl.when(jnp.logical_not(even))
        def _():
            window_copy(g, 0, 0, c + 1).wait_recv()

    partners = [
        {"fc": (c + n // 2) % n},
        {"fc": c + 1 - 2 * (c % 2)},
        {"fr": (r + nr // 2) % nr},
        {"fr": r + 1 - 2 * (r % 2)},
    ]

    def level_copy(level, k):
        return pltpu.make_async_remote_copy(
            src_ref=front.at[k, pl.ds(0, block)] if level else front_hbm.at[pl.ds(0, block), columns(k)],
            dst_ref=received.at[level, k],
            send_sem=level_send.at[level, k], recv_sem=level_recv.at[level, k],
            device_id=partners[level], device_id_type=MESH,
        )

    def panel_copy(k):
        part = pl.ds(pl.multiple_of(k * WIDTH, WIDTH), WIDTH)
        return pltpu.make_async_copy(panels_hbm.at[:, part], panels.at[:, part], panel_sem.at[k])

    def out_copy(k):
        return pltpu.make_async_copy(front.at[k], out_hbm.at[:, columns(k)], out_sem.at[k])

    def start_first_level(first, end):
        @pl.loop(first, end)
        def _(k):
            level_copy(0, k).start()

    @pl.when(c == 0)
    def _():
        chain(0)

    @pl.loop(0, chunks)
    def _(k):
        front_copy(k).wait()

    upper = c >= n // 2
    steps = pw // PIVOT
    hops = c // 2 + c % 2

    def relay_step(g):
        return g + hops

    @pl.when(upper)
    def _():
        start_first_level(0, OPEN)

    @pl.loop(0, chunks)
    def _(k):
        panel_copy(k).start()

    for level in range(levels):
        wanted = maps_ref[pl.ds(level, 1), :]
        index = lax.broadcasted_iota(jnp.int32, (block, block), 0)
        move = jnp.where(index == wanted, 1.0, 0.0).T.astype(BF16)
        moves[level] = jnp.concatenate([move, move], axis=1)

    diag_load.wait()
    for copy in diag_copies:
        copy.wait()
    transposed = gathered[...]
    symmetric = 0.5 * (transposed + transposed.T)
    sub = lax.broadcasted_iota(jnp.int32, symmetric.shape, 0)
    lane = lax.broadcasted_iota(jnp.int32, symmetric.shape, 1)
    diagonal = jnp.where(sub == lane, symmetric, 0.0)
    scale_row = lax.rsqrt(jnp.sum(diagonal, axis=0, keepdims=True))
    scale_column = lax.rsqrt(jnp.sum(diagonal, axis=1, keepdims=True))
    work[...] = symmetric * scale_row * scale_column
    shared[r, pl.ds(pw, 8), :] = jnp.broadcast_to(scale_row, (8, pw))

    @pl.loop(0, steps)
    def _(i):
        pivot_step(work)

        for g in range(groups):
            @pl.when(jnp.logical_and(c > 0, i == relay_step(g)))
            def _():
                chain(g)

            @pl.when(jnp.logical_and(c == 0, i == steps - groups + g))
            def _():
                across(g, start)

            if g:
                @pl.when(jnp.logical_and(c == 0, i == g - 1))
                def _():
                    forwards(g - 1, wait_send)
                    chain(g)

        @pl.when(jnp.logical_and(upper, i + OPEN < chunks))
        def _():
            level_copy(0, i + OPEN).start()

        @pl.when(jnp.logical_and(jnp.logical_not(upper), i >= HOLD))
        def _():
            level_copy(0, i - HOLD).start()

    shared[r, pl.ds(0, pw), :] = work[...]
    def inv_copy(index, slot, target):
        return pltpu.make_async_remote_copy(
            src_ref=shared.at[slot], dst_ref=shared.at[slot],
            send_sem=inv_send.at[index], recv_sem=inv_recv.at[index],
            device_id=target, device_id_type=MESH,
        )

    far, near = partners[2], partners[3]
    far_copy = inv_copy(0, r, far)
    near_copy = inv_copy(1, r, near)
    pass_copy = inv_copy(2, far["fr"], near)
    far_copy.start()
    near_copy.start()
    for g in range(groups):
        @pl.when(jnp.logical_and(c > 0, relay_step(g) >= steps))
        def _():
            chain(g)

    @pl.when(c == 0)
    def _():
        forwards(groups - 1, wait_send)

    @pl.when(upper)
    def _():
        start_first_level(min(steps + OPEN, chunks), chunks)

    @pl.when(jnp.logical_not(upper))
    def _():
        start_first_level(steps - HOLD, chunks)

    far_copy.wait_recv()
    pass_copy.start()
    for g in range(groups):
        rest_of(g)
    far_copy.wait_send()
    near_copy.wait()
    pass_copy.wait()

    def scaled(x, level):
        return x * shared[level, pl.ds(pw, 1), :]

    for level in range(levels):
        x_high, x_low = split(scaled(window[level], level))
        high, low = split(shared[level, pl.ds(0, pw), :])
        s = jnp.dot(
            jnp.concatenate([x_high, x_low, x_high], axis=1),
            jnp.concatenate([high, high, low], axis=0),
            preferred_element_type=F32,
        )
        high, low = split(s)
        factors[level] = jnp.concatenate([high, low, high], axis=1)
    def update(level, k):
        high, low = split(scaled(panels[level, columns(k), :], level))
        return dot_t(factors[level], jnp.concatenate([high, high, low], axis=1))

    def arrive(level, k):
        if level == 0:
            panel_copy(k).wait()
            level_copy(level, k).wait_recv()
        else:
            level_copy(level, k).wait()

    def stage(level, k):
        total = update(level, k)
        top, below = pl.ds(0, block), pl.ds(block, rows - block)
        pair = jnp.concatenate(split(received[level, k]), axis=0)
        moved = jnp.dot(moves[level], pair, preferred_element_type=F32)
        front[k, top, :] = front[k, top, :] + moved - total[:block]
        front[k, below, :] = front[k, below, :] - total[block:]

    def leave(level, k):
        if level + 1 < levels:
            level_copy(level + 1, k).start()
        else:
            out_copy(k).start()

    marks = sorted({SKEW * level + end for level in range(levels) for end in (0, chunks)})
    for first, end in zip(marks, marks[1:]):
        active = [x for x in reversed(range(levels)) if SKEW * x <= first < chunks + SKEW * x]

        @pl.loop(first, end)
        def _(t, active=active):
            for act in (arrive, stage, leave):
                for level in active:
                    act(level, t - SKEW * level)

    for g in range(groups):
        @pl.when(c > 0)
        def _():
            forwards(g, wait_send)

        across(g, wait_send)

    @pl.loop(0, chunks)
    def _(k):
        out_copy(k).wait()
        level_copy(0, k).wait_send()


def body(front_slab, panels, diagonal_blocks, extend_maps):
    rows, cols = front_slab.shape
    levels, _, pw = panels.shape
    block = extend_maps.shape[3]
    n, nr = lax.axis_size("fc"), lax.axis_size("fr")
    chunks, groups = cols // WIDTH, rows // block
    mine = lax.dynamic_index_in_dim(diagonal_blocks, lax.axis_index("fr"), 0, keepdims=False).T
    anywhere = pl.BlockSpec(memory_space=pl.ANY)
    dma = pltpu.SemaphoreType.DMA
    return pl.pallas_call(
        functools.partial(kernel, n, nr),
        out_shape=jax.ShapeDtypeStruct((rows, cols), F32),
        in_specs=[anywhere, anywhere, anywhere, pl.BlockSpec(memory_space=pltpu.VMEM)],
        out_specs=anywhere,
        scratch_shapes=[
            pltpu.VMEM((chunks, rows, WIDTH), F32),
            pltpu.VMEM(panels.shape, F32),
            pltpu.VMEM((pw, pw), F32),
            pltpu.VMEM((pw, pw), F32),
            pltpu.VMEM((levels, pw + 8, pw), F32),
            pltpu.VMEM((levels, rows, pw), F32),
            pltpu.VMEM((levels, rows, 3 * pw), BF16),
            pltpu.VMEM((levels, block, 2 * block), BF16),
            pltpu.VMEM((levels, chunks, block, WIDTH), F32),
            dma((n - 1,)),
            dma((n - 1,)),
            dma((groups, 2, 2)),
            dma((groups, 2)),
            dma((groups,)),
            dma((nr - 1,)),
            dma((nr - 1,)),
            dma((levels, chunks)),
            dma((levels, chunks)),
            dma,
            dma((chunks,)),
            dma((chunks,)),
            dma((chunks,)),
        ],
        compiler_params=pltpu.CompilerParams(
            collective_id=0, has_side_effects=True, vmem_limit_bytes=50 * 2**20
        ),
        cost_estimate=pl.CostEstimate(
            flops=6 * rows * cols * levels * pw, bytes_accessed=8 * rows * cols + 4 * panels.size, transcendentals=0
        ),
    )(front_slab, panels, mine, extend_maps.reshape(levels, block))


def solution(mesh):
    in_specs = (P("fr", "fc"), P(None, "fc", None), P(None, None, "fc"), P(None, "fr", "fc", None))
    return jax.shard_map(body, mesh=mesh, in_specs=in_specs, out_specs=P("fr", "fc"), check_vma=False)
```
